32 devices in a mesh: blk: 8 (over z, core), grp: 4 (over y, x).
Axes of the slice: x: 2, y: 2, z: 4, core: 2. Of those that a mesh axis runs over, the one named last changes fastest.
Arguments:
- queries: bfloat16 [64, 5120], P(('grp', 'blk')), parts along dimension 0, may hold values from -28 to 28
- cache_keys: bfloat16 [256, 128, 1024], P(('grp', 'blk')), parts along dimension 0, may hold values from -24 to 24
- pool_values_prior: bfloat16 [256, 128, 1024], P(('grp', 'blk')), parts along dimension 0, may hold values from -6 to 6
- prefill_keys: bfloat16 [64, 128, 1024], P(('grp', 'blk')), parts along dimension 0, may hold values from -6 to 6
- prefill_values: bfloat16 [64, 128, 1024], P(('grp', 'blk')), parts along dimension 0, may hold values from -6 to 6
- context_lengths: int32 [16], P('grp'), parts along dimension 0, may hold values from 516 to 2048, as said below
- block_table: int32 [16, 16], P('grp'), parts along dimension 0, may hold values from 0 to 63, as said below
- spill_slots: int32 [64], P('grp'), parts along dimension 0, may hold values from 0 to 63, as said below
Outputs:
- attended: bfloat16 [64, 5120], P(('grp', 'blk')), parts along dimension 0
- pool_keys: bfloat16 [256, 128, 1024], P(('grp', 'blk')), parts along dimension 0
- pool_values: bfloat16 [256, 128, 1024], P(('grp', 'blk')), parts along dimension 0
The draws below stay inside these ranges and needn't reach their ends.
There are 4 independent parts, one for each index of `grp`. The reference program is written for one: setup_inputs(seed, part) draws one part's arguments, and reference() takes and returns one part's arrays. A program takes and returns all parts, laid end to end along the dimension named above; each array names one. Nothing has to cross between parts.
Inputs may be any that keep to these rules, and one draw needn't show every extreme that they name: Every pool block appears exactly once in block_table, so each request owns 16 blocks. `spill_slots`: distinct pool blocks; exactly 2 of them lie in each rank's range of 8 blocks, and each stands among the first 4 columns of some row of block_table. `context_lengths`: some request has 2048 tokens.
All inputs are finite; a program needn't handle non-finite values.
Results may differ from the reference program's by a relative error of at most 0.0045.
Values may be sent and summed in bfloat16 or wider, within the bound.
A program may use at most 128 MiB of HBM per device.

```python
import jax
import jax.numpy as jnp
from jax import lax

QUERY_HEADS = 40
KEY_VALUE_HEADS = 8
HEAD_SIZE = 128
BLOCK_TOKENS = 128
STEPS = 4
REQ = 4
PF_DEV = 2
RANK_BLOCKS = 8
POOL_BLOCKS = 64
MAXB = 16
QUERY_ROWS = 16
PREFILL_BLOCKS = 16
N_BLK = 8


def placement(key):
    ranks = POOL_BLOCKS // RANK_BLOCKS
    rank_keys = jax.random.split(jax.random.fold_in(key, 101), ranks)
    within = jax.vmap(lambda single: jax.random.permutation(single, RANK_BLOCKS))(rank_keys).astype(jnp.int32)
    base = (jnp.arange(ranks, dtype=jnp.int32) * RANK_BLOCKS)[:, None]
    chosen = (base + within[:, :PF_DEV]).reshape(-1)
    others = (base + within[:, PF_DEV:]).reshape(-1)
    chosen = jax.random.permutation(jax.random.fold_in(key, 102), chosen).astype(jnp.int32)
    others = jax.random.permutation(jax.random.fold_in(key, 103), others).astype(jnp.int32)
    leading = PREFILL_BLOCKS // REQ
    table = jnp.concatenate([chosen.reshape(REQ, leading), others.reshape(REQ, MAXB - leading)], axis=1)
    return (table.astype(jnp.int32), chosen)


def draw_block_table(key, part):
    table, chosen = placement(key)
    return table


def draw_spill_slots(key, part):
    table, chosen = placement(key)
    return chosen


def draw_context_lengths(key, part):
    key = jax.random.fold_in(key, 5)
    first_block, second = jax.random.split(key)
    lengths = jax.random.randint(first_block, (REQ,), PREFILL_BLOCKS // REQ * BLOCK_TOKENS + STEPS, MAXB * BLOCK_TOKENS + 1)
    longest = jax.random.randint(second, (), 0, REQ)
    return jnp.where(jnp.arange(REQ) == longest, MAXB * BLOCK_TOKENS, lengths).astype(jnp.int32)


def draw_cache_keys(key, part):
    key = jax.random.fold_in(key, 7)
    first_block = jax.random.fold_in(key, 0)
    random_offset = jnp.clip(jax.random.normal(first_block, (POOL_BLOCKS, BLOCK_TOKENS, KEY_VALUE_HEADS * HEAD_SIZE), jnp.float32), -3.5, 3.5)
    return random_offset.astype(jnp.bfloat16)


def draw_queries(key, part):
    key = jax.random.fold_in(key, 9)
    first_block = jax.random.fold_in(key, 0)
    random_offset = jnp.clip(jax.random.normal(first_block, (QUERY_ROWS, QUERY_HEADS * HEAD_SIZE), jnp.float32), -3.5, 3.5)
    return random_offset.astype(jnp.bfloat16)


def level_of(own_key, shape, cuts, least, high):
    loudness, own = 1.0, jax.random.fold_in(own_key, 6)
    for axis_at, shards_of in cuts:
        steps = jnp.exp(jax.random.uniform(jax.random.fold_in(own, axis_at), (shards_of,), jnp.float32, least / len(cuts), high / len(cuts)))
        loudness = loudness * jnp.repeat(steps, shape[axis_at] // shards_of).reshape([-1 if axis == axis_at else 1 for axis in range(len(shape))])
    return loudness


def scatter_about(rng, dims, scale, most, cuts=(), kind=jnp.bfloat16):
    values = scale * jax.random.normal(rng, dims, jnp.float32)
    if cuts:
        values = values * level_of(rng, dims, cuts, -0.22, 0.18)
    return jnp.clip(values, -most, most).astype(kind)


def setup_inputs(seed: int = 0, part: int = 0) -> dict:
    keys = jax.random.split(jax.random.key(seed), 9)
    part_splits = jax.random.split(jax.random.fold_in(keys[8], part), 9)
    queries = draw_queries(jax.random.fold_in(jax.random.fold_in(keys[8], part), 71), part)
    cache_keys = draw_cache_keys(jax.random.fold_in(jax.random.fold_in(keys[8], part), 71), part)
    pool_values_prior = scatter_about(part_splits[2], (POOL_BLOCKS, BLOCK_TOKENS, KEY_VALUE_HEADS * HEAD_SIZE), 1.0, 6.0, ((0, 8),))
    prefill_keys = scatter_about(part_splits[3], (PREFILL_BLOCKS, BLOCK_TOKENS, KEY_VALUE_HEADS * HEAD_SIZE), 1.0, 6.0, ((0, 8),))
    prefill_values = scatter_about(part_splits[4], (PREFILL_BLOCKS, BLOCK_TOKENS, KEY_VALUE_HEADS * HEAD_SIZE), 1.0, 6.0, ((0, 8),))
    context_lengths = draw_context_lengths(jax.random.fold_in(jax.random.fold_in(keys[8], part), 71), part)
    block_table = draw_block_table(jax.random.fold_in(jax.random.fold_in(keys[8], part), 71), part)
    spill_slots = draw_spill_slots(jax.random.fold_in(jax.random.fold_in(keys[8], part), 71), part)
    return {"queries": queries, "cache_keys": cache_keys, "pool_values_prior": pool_values_prior, "prefill_keys": prefill_keys, "prefill_values": prefill_values, "context_lengths": context_lengths, "block_table": block_table, "spill_slots": spill_slots}


NEGATIVE_LARGE = -1.0e30


def merge_state(running, incoming):
    run_max, run_sum, run_out = running
    new_max, new_sum, new_out = incoming
    largest = jnp.maximum(run_max, new_max)
    keep = jnp.exp(run_max - largest)
    take = jnp.exp(new_max - largest)
    return (largest, run_sum * keep + new_sum * take, run_out * keep[..., None] + new_out * take[..., None])


def rank_partial(queries, keys_of_block, values_of_block, owner, limit):
    head_groups = QUERY_HEADS // KEY_VALUE_HEADS
    row_ids = jnp.arange(QUERY_ROWS, dtype=jnp.int32)
    step_of = row_ids // REQ
    request_of = row_ids % REQ
    query_head_rows = queries.astype(jnp.float32).reshape(QUERY_ROWS, KEY_VALUE_HEADS, head_groups, HEAD_SIZE)
    key_head_rows = keys_of_block.astype(jnp.float32).reshape(RANK_BLOCKS, BLOCK_TOKENS, KEY_VALUE_HEADS, HEAD_SIZE)
    scores = jnp.einsum("rhgd,sthd->rhgst", query_head_rows, key_head_rows, precision=lax.Precision.HIGHEST) * (HEAD_SIZE ** -0.5)
    bound = limit[None, :] - (STEPS - 1) + step_of[:, None]
    visible = jnp.arange(BLOCK_TOKENS, dtype=jnp.int32)[None, None, :] < bound[:, :, None]
    visible = visible & (owner[None, :] == request_of[:, None])[:, :, None]
    visible = visible[:, None, None]
    masked = jnp.where(visible, scores, NEGATIVE_LARGE)
    row_max = jnp.max(masked, axis=(-2, -1))
    weights = jnp.where(visible, jnp.exp(masked - row_max[..., None, None]), jnp.float32(0.0))
    row_sum = jnp.sum(weights, axis=(-2, -1))
    probs = weights.astype(jnp.bfloat16).astype(jnp.float32)
    value_head_rows = values_of_block.astype(jnp.float32).reshape(RANK_BLOCKS, BLOCK_TOKENS, KEY_VALUE_HEADS, HEAD_SIZE)
    row_out = jnp.einsum("rhgst,sthd->rhgd", probs, value_head_rows, precision=lax.Precision.HIGHEST)
    return (row_max, row_sum, row_out)


def reference(queries, cache_keys, pool_values_prior, prefill_keys, prefill_values, context_lengths, block_table, spill_slots):
    pool_keys = cache_keys.at[spill_slots].set(prefill_keys)
    pool_values = pool_values_prior.at[spill_slots].set(prefill_values)
    blocks = jnp.arange(POOL_BLOCKS, dtype=jnp.int32)
    match = block_table[:, :, None] == blocks[None, None, :]
    request_ids = jnp.arange(REQ, dtype=jnp.int32)[:, None, None]
    owner = jnp.sum(jnp.where(match, request_ids, 0), axis=(0, 1)).astype(jnp.int32)
    column = jnp.arange(MAXB, dtype=jnp.int32)[None, :, None]
    limit = jnp.sum(jnp.where(match, context_lengths[:, None, None] - column * BLOCK_TOKENS, 0), axis=(0, 1)).astype(jnp.int32)
    head_groups = QUERY_HEADS // KEY_VALUE_HEADS
    start_offset = (jnp.full((QUERY_ROWS, KEY_VALUE_HEADS, head_groups), NEGATIVE_LARGE, jnp.float32),
             jnp.zeros((QUERY_ROWS, KEY_VALUE_HEADS, head_groups), jnp.float32),
             jnp.zeros((QUERY_ROWS, KEY_VALUE_HEADS, head_groups, HEAD_SIZE), jnp.float32))

    def visit(running, rank):
        first_block = (rank * RANK_BLOCKS).astype(jnp.int32)
        keys_of_block = lax.dynamic_slice_in_dim(pool_keys, first_block, RANK_BLOCKS, 0)
        values_of_block = lax.dynamic_slice_in_dim(pool_values, first_block, RANK_BLOCKS, 0)
        block_owner = lax.dynamic_slice_in_dim(owner, first_block, RANK_BLOCKS, 0)
        block_limit = lax.dynamic_slice_in_dim(limit, first_block, RANK_BLOCKS, 0)
        partial_state = rank_partial(queries, keys_of_block, values_of_block, block_owner, block_limit)
        return merge_state(running, partial_state), None

    final, unused = lax.scan(visit, start_offset, jnp.arange(N_BLK, dtype=jnp.int32))
    attended = final[2] / final[1][..., None]
    attended = attended.reshape(QUERY_ROWS, QUERY_HEADS * HEAD_SIZE).astype(jnp.bfloat16)
    return (attended, pool_keys, pool_values)
```

```python
import functools

import jax
import jax.numpy as jnp
from jax import lax
from jax.experimental import pallas as pl
from jax.experimental.pallas import tpu as pltpu
from jax.sharding import PartitionSpec as P

QUERY_HEADS = 40
KV = 8
GROUPS = QUERY_HEADS // KV
HEAD = 128
STEPS = 4
REQ = 4
ROWS = 16
PIECES = 4
HEADS_PER_STEP = 2
LOW = -1e30
FAR = 1 << 24
MESH = pl.DeviceIdType.MESH


def lane_plan(spill, chips, z, lanes, chip_blocks, rank_slots):
    total = chips * chip_blocks
    rank_of = [spill[b] // rank_slots for b in range(total)]
    chip_of = [r // 2 for r in rank_of]
    sends, arrivals = [], []
    for way in range(2):
        dest = chip_of if way == 0 else [chips - 1 - c for c in chip_of]
        place = z if way == 0 else chips - 1 - z
        lane_dest = [jnp.int32(-1)] * lanes
        lane_block = [jnp.int32(-1)] * lanes
        send = [jnp.int32(chip_blocks)] * lanes
        arrive = [jnp.int32(-1)] * lanes
        for n in range(chips):
            here = place == n
            if n > 0:
                arrive = [jnp.where(here, lane_block[l], arrive[l]) for l in range(lanes)]
            if n == chips - 1:
                break
            first = (n if way == 0 else chips - 1 - n) * chip_blocks
            left = [dest[first + i] > n for i in range(chip_blocks)]
            for l in reversed(range(min(lanes, chip_blocks * (n + 1)))):
                pick, pick_dest = jnp.int32(chip_blocks), jnp.int32(-1)
                for i in reversed(range(chip_blocks)):
                    pick = jnp.where(left[i], i, pick)
                    pick_dest = jnp.where(left[i], dest[first + i], pick_dest)
                take = (lane_dest[l] <= n) & (pick < chip_blocks)
                left = [left[i] & jnp.logical_not(take & (pick == i)) for i in range(chip_blocks)]
                lane_dest[l] = jnp.where(take, pick_dest, lane_dest[l])
                lane_block[l] = jnp.where(take, first + pick, lane_block[l])
                send[l] = jnp.where(here & take, pick, send[l])
        sends.append(send)
        arrivals.append(arrive)
    return rank_of, sends, arrivals


def blocks_for(rank, rank_of, per_rank):
    found = [jnp.int32(0)] * per_rank
    count = jnp.int32(0)
    for b, target in enumerate(rank_of):
        hit = target == rank
        found = [jnp.where(hit & (count == q), b, found[q]) for q in range(per_rank)]
        count = count + hit.astype(jnp.int32)
    return found


def exchange_kernel(
    chips, lanes, limits, spill, q_ref, pk, pv, ck, cv,
    att, newk, newv,
    kall, vall, own, arr, snd, fin, pout, pin, qg, bias, part, lse, pin_o, pin_l, mo, ml, ro, rl, sched,
    loc, ex_s, ex_r, q_s, q_r, lane_s, lane_r, s1_s, s1_r, s2_s, s2_r, fx_s, fx_r, out_s,
):
    rank_slots, tokens, width = ck.shape
    per_rank = pk.shape[0]
    chip_blocks = 2 * per_rank
    blocks = rank_slots + per_rank
    rows_here = STEPS * REQ // (2 * chips)
    piece = tokens // PIECES
    me = lax.axis_index("blk")
    z = me // 2
    core = lax.rem(me, 2)
    partner = 2 * z + 1 - core

    def remote(src, dst, s, r, rank):
        return pltpu.make_async_remote_copy(
            src_ref=src, dst_ref=dst, send_sem=s, recv_sem=r, device_id={"blk": rank}, device_id_type=MESH
        )

    load_kp = pltpu.make_async_copy(pk, kall.at[pl.ds(rank_slots, per_rank)], loc.at[0])
    load_vp = pltpu.make_async_copy(pv, vall.at[pl.ds(rank_slots, per_rank)], loc.at[1])
    load_kc = pltpu.make_async_copy(ck, kall.at[pl.ds(0, rank_slots)], loc.at[2])
    load_vc = pltpu.make_async_copy(cv, vall.at[pl.ds(0, rank_slots)], loc.at[3])
    own_mine = own.at[pl.ds(core * per_rank, per_rank)]

    @pl.when(core == 0)
    def _():
        pltpu.make_async_copy(pk, own_mine, loc.at[4]).start()

    @pl.when(core == 1)
    def _():
        pltpu.make_async_copy(pv, own_mine, loc.at[4]).start()

    load_kp.start()
    load_vp.start()
    load_kc.start()
    load_vc.start()

    barrier = pltpu.get_barrier_semaphore()
    pl.semaphore_signal(barrier, inc=1, device_id={"blk": partner}, device_id_type=MESH)
    for off in range(1, chips):
        peer = 2 * lax.rem(z + off, chips) + core
        pl.semaphore_signal(barrier, inc=1, device_id={"blk": peer}, device_id_type=MESH)
    pl.semaphore_wait(barrier, chips)

    @pl.when(core == 0)
    def _():
        remote(pv, own_mine, ex_s, ex_r, partner).start()

    @pl.when(core == 1)
    def _():
        remote(pk, own_mine, ex_s, ex_r, partner).start()

    mine = core * chips + z
    q_copies = [remote(q_ref, qg.at[mine], q_s.at[0], q_r.at[mine], partner)]
    for off in range(1, chips):
        peer = 2 * lax.rem(z + off, chips) + core
        q_copies.append(remote(q_ref, qg.at[mine], q_s.at[off], q_r.at[mine], peer))
    for copy in q_copies:
        copy.start()
    qg[mine] = q_ref[...]

    rank_of, sends, arrivals = lane_plan(spill, chips, z, lanes, chip_blocks, rank_slots)
    for way in range(2):
        for l in range(lanes):
            sched[way, l] = sends[way][l]

    pltpu.make_async_copy(pk, own_mine, loc.at[4]).wait()
    own_other = own.at[pl.ds((1 - core) * per_rank, per_rank)]
    arrived = remote(pk, own_other, ex_s, ex_r, partner)
    arrived.wait_recv()

    low_half = z < chips // 2
    near = jnp.where(low_half, z, chips - 1 - z)
    far = chips - 1 - near
    near_way = jnp.where(low_half, 0, 1)
    far_way = 1 - near_way
    near_next = 2 * jnp.where(low_half, z + 1, z - 1) + core
    far_next = 2 * jnp.where(low_half, jnp.maximum(z - 1, 0), jnp.minimum(z + 1, chips - 1)) + core

    def lane_copy(way, l, p, rank):
        rows = pl.ds(p * piece, piece)
        return remote(
            snd.at[way, l, rows], arr.at[way, l, rows], lane_s.at[way, l, p], lane_r.at[way, l, p], rank
        )

    def compose(way, l, p):
        rows = pl.ds(p * piece, piece)
        pick = sched[way, l]
        snd[way, l, rows] = lax.select(
            pick == chip_blocks, arr[way, l, rows], own[jnp.minimum(pick, chip_blocks - 1), rows]
        )

    def compose_own(way, l, p):
        rows = pl.ds(p * piece, piece)
        snd[way, l, rows] = own[jnp.minimum(sched[way, l], chip_blocks - 1), rows]

    def near_step(i):
        l = lanes - 1 - i
        passing = l < chip_blocks * near
        starting = jnp.logical_not(passing) & (l < chip_blocks * (near + 1))

        @pl.when((l + 2 < lanes) & (l + 2 < chip_blocks * (near + 1)))
        def _():
            for p in range(PIECES):
                lane_copy(near_way, l + 2, p, near_next).wait_send()

        @pl.when(passing)
        def _():
            for p in range(PIECES):
                lane_copy(near_way, l, p, near_next).wait_recv()
                compose(near_way, l, p)
                lane_copy(near_way, l, p, near_next).start()

        @pl.when(starting)
        def _():
            for p in range(PIECES):
                compose_own(near_way, l, p)
                lane_copy(near_way, l, p, near_next).start()

    def far_step(i):
        l = lanes - 1 - i

        @pl.when(far < chips - 1)
        def _():
            for p in range(PIECES):
                lane_copy(far_way, l, p, far_next).wait_recv()
                compose(far_way, l, p)
                lane_copy(far_way, l, p, far_next).start()

    def attend(h):
        cols = pl.ds(pl.multiple_of(h * HEAD, HEAD), HEAD)
        q = qg[:, h].reshape(2 * chips * ROWS, HEAD)
        k = kall[:, :, cols].reshape(blocks * tokens, HEAD)
        v = vall[:, :, cols].reshape(blocks * tokens, HEAD)
        s = lax.dot_general(q, k, (((1,), (1,)), ((), ())), preferred_element_type=jnp.float32)
        s = s * HEAD ** (-0.5) + bias[...]
        m = jnp.max(s, axis=1, keepdims=True)
        w = jnp.exp(s - m)
        total = jnp.sum(w, axis=1, keepdims=True)
        o = jnp.dot(w.astype(jnp.bfloat16), v, preferred_element_type=jnp.float32) / total
        part[:, h] = o.astype(jnp.bfloat16).reshape(2 * chips, ROWS, HEAD)
        lane = lax.broadcasted_iota(jnp.int32, (2 * chips, ROWS, HEAD), 2)
        level = (m + jnp.log(total)).reshape(2 * chips, ROWS, 1)
        lse[...] = jnp.where(lane == h, level, lse[...])

    near_step(0)

    for off in range(1, chips):
        other = core * chips + lax.rem(z + off, chips)
        remote(q_ref, qg.at[other], q_s.at[0], q_r.at[other], partner).wait_recv()
        remote(qg.at[other], qg.at[other], q_s.at[chips - 1 + off], q_r.at[other], partner).start()

    row_count = 2 * chips * ROWS
    row = lax.broadcasted_iota(jnp.int32, (row_count, HEAD), 0)
    slot, inner = row // ROWS, row % ROWS
    rank_row = 2 * (slot % chips) + slot // chips
    row_id = rank_row * rows_here + inner % rows_here
    valid = inner < GROUPS * rows_here
    step, request = row_id // REQ, row_id % REQ
    token = lax.broadcasted_iota(jnp.int32, (row_count, HEAD), 1)
    edge = jnp.where(valid, token + (STEPS - 1) - step, FAR)
    for s in range(blocks):
        bound = jnp.where(request == 0, limits[0, s], -FAR)
        for r in range(1, REQ):
            bound = jnp.where(request == r, limits[r, s], bound)
        bias[:, pl.ds(s * tokens, tokens)] = jnp.where(edge < bound, 0.0, LOW).astype(jnp.float32)
    lse[...] = jnp.zeros_like(lse)

    load_kp.wait()
    load_vp.wait()
    load_kc.wait()
    load_vc.wait()
    for zz in range(chips):
        other = (1 - core) * chips + zz
        remote(q_ref, qg.at[other], q_s.at[0], q_r.at[other], partner).wait_recv()

    attending = KV // HEADS_PER_STEP

    def mixed(i, carry):
        near_step(i)
        far_step(i - 1)
        for e in range(HEADS_PER_STEP):
            attend((i - 1) * HEADS_PER_STEP + e)
        return carry

    lax.fori_loop(1, 1 + attending, mixed, 0)

    theirs = pl.ds((1 - core) * chips, chips)
    s1_o = remote(part.at[theirs], pin_o, s1_s.at[0], s1_r.at[0], partner)
    s1_l = remote(lse.at[theirs], pin_l, s1_s.at[1], s1_r.at[1], partner)
    s1_o.start()
    s1_l.start()
    near_step(1 + attending)
    far_step(attending)
    s1_o.wait_recv()
    s1_l.wait_recv()

    ours = pl.ds(core * chips, chips)
    level_a, level_b = lse[ours], pin_l[...]
    top = jnp.maximum(level_a, level_b)
    ea, eb = jnp.exp(level_a - top), jnp.exp(level_b - top)
    both = ea + eb
    ml[...] = top + jnp.log(both)
    wa, wb = ea / both, eb / both
    for h in range(KV):
        pa = part[ours, h].astype(jnp.float32)
        pb = pin_o[:, h].astype(jnp.float32)
        mo[:, h] = (pa * wa[:, :, h : h + 1] + pb * wb[:, :, h : h + 1]).astype(jnp.bfloat16)
    s2 = []
    for off in range(1, chips):
        to = lax.rem(z + off, chips)
        s2.append(remote(mo.at[to], ro.at[z], s2_s.at[0, off], s2_r.at[0, z], 2 * to + core))
        s2.append(remote(ml.at[to], rl.at[z], s2_s.at[1, off], s2_r.at[1, z], 2 * to + core))
    for copy in s2:
        copy.start()
    ro[z] = mo[z]
    rl[z] = ml[z]

    def moving(i, carry):
        near_step(i)
        far_step(i - 1)
        return carry

    lax.fori_loop(2 + attending, lanes, moving, 0)
    far_step(lanes - 1)

    for off in range(1, chips):
        source = lax.rem(z + off, chips)
        remote(mo.at[source], ro.at[source], s2_s.at[0, off], s2_r.at[0, source], partner).wait_recv()
        remote(ml.at[source], rl.at[source], s2_s.at[1, off], s2_r.at[1, source], partner).wait_recv()
    levels = rl[...]
    top = jnp.max(levels, axis=0, keepdims=True)
    shares = jnp.exp(levels - top)
    shares = shares / jnp.sum(shares, axis=0, keepdims=True)
    for h in range(KV):
        att[h] = jnp.sum(ro[:, h].astype(jnp.float32) * shares[:, :, h : h + 1], axis=0).astype(jnp.bfloat16)

    @pl.when(far == chips - 1)
    def _():
        def drain(i, carry):
            for p in range(PIECES):
                lane_copy(far_way, lanes - 1 - i, p, far_next).wait_recv()
            return carry

        lax.fori_loop(0, lanes, drain, 0)

    def gathered(b, q, target):
        at_home = b // chip_blocks == z
        index = jnp.clip(b - z * chip_blocks, 0, chip_blocks - 1)
        way_of, lane_of = jnp.int32(0), jnp.int32(0)
        for way in range(2):
            for l in range(lanes):
                hit = arrivals[way][l] == b
                way_of = jnp.where(hit, way, way_of)
                lane_of = jnp.where(hit, l, lane_of)
        target[q] = lax.select(at_home, own[index], arr[way_of, lane_of])

    for q, b in enumerate(blocks_for(partner, rank_of, per_rank)):
        gathered(b, q, pout)
    handed = remote(pout, pin, fx_s, fx_r, partner)
    handed.start()
    for q, b in enumerate(blocks_for(me, rank_of, per_rank)):
        gathered(b, q, fin)

    @pl.when(core == 0)
    def _():
        pltpu.make_async_copy(fin, newk, out_s.at[0]).start()

    @pl.when(core == 1)
    def _():
        pltpu.make_async_copy(fin, newv, out_s.at[0]).start()

    handed.wait_recv()

    @pl.when(core == 0)
    def _():
        pltpu.make_async_copy(pin, newv, out_s.at[1]).start()

    @pl.when(core == 1)
    def _():
        pltpu.make_async_copy(pin, newk, out_s.at[1]).start()

    handed.wait_send()
    arrived.wait_send()
    s1_o.wait_send()
    s1_l.wait_send()
    for copy in s2:
        copy.wait_send()
    for off in range(2 * chips - 1):
        remote(q_ref, qg.at[mine], q_s.at[off], q_r.at[mine], partner).wait_send()
    for l in range(2):
        @pl.when(l < chip_blocks * (near + 1))
        def _():
            for p in range(PIECES):
                lane_copy(near_way, l, p, near_next).wait_send()

    @pl.when(far < chips - 1)
    def _():
        def sent(i, carry):
            for p in range(PIECES):
                lane_copy(far_way, i, p, far_next).wait_send()
            return carry

        lax.fori_loop(0, lanes, sent, 0)

    pltpu.make_async_copy(fin, newk, out_s.at[0]).wait()
    pltpu.make_async_copy(pin, newv, out_s.at[1]).wait()


def place_kernel(spill, first_ref, ck, cv, newk, newv, att_in, pool_k, pool_v, att_out, sem, att_sem):
    rank_slots = ck.shape[0]
    first = first_ref[0]
    att_copy = pltpu.make_async_copy(att_in, att_out, att_sem)
    att_copy.start()
    filled = [jnp.bool_(False)] * rank_slots
    count = jnp.int32(0)
    for b in range(spill.shape[0]):
        at = spill[b] - first
        mine = (at >= 0) & (at < rank_slots)
        filled = [filled[j] | (at == j) for j in range(rank_slots)]
        here, which = jnp.clip(at, 0, rank_slots - 1), jnp.minimum(count, newk.shape[0] - 1)

        @pl.when(mine)
        def _():
            pltpu.make_async_copy(newk.at[which], pool_k.at[here], sem.at[0, here]).start()
            pltpu.make_async_copy(newv.at[which], pool_v.at[here], sem.at[1, here]).start()

        count = count + mine.astype(jnp.int32)
    for j in range(rank_slots):
        @pl.when(jnp.logical_not(filled[j]))
        def _():
            pltpu.make_async_copy(ck.at[j], pool_k.at[j], sem.at[0, j]).start()
            pltpu.make_async_copy(cv.at[j], pool_v.at[j], sem.at[1, j]).start()

    for j in range(rank_slots):
        pltpu.make_async_copy(ck.at[j], pool_k.at[j], sem.at[0, j]).wait()
        pltpu.make_async_copy(cv.at[j], pool_v.at[j], sem.at[1, j]).wait()
    att_copy.wait()


def per_device(
    queries, cache_keys, pool_values_prior, prefill_keys, prefill_values, context_lengths, block_table, spill_slots
):
    ranks = lax.axis_size("blk")
    chips = ranks // 2
    me = lax.axis_index("blk")
    rank_slots, tokens, width = cache_keys.shape
    per_rank = prefill_keys.shape[0]
    chip_blocks = 2 * per_rank
    blocks = rank_slots + per_rank
    lanes = chip_blocks * (chips // 2)
    rows_here, query_width = queries.shape
    first = me * rank_slots

    held = first + jnp.arange(rank_slots, dtype=jnp.int32)
    gone = jnp.any(held[:, None] == spill_slots[None, :], axis=1)
    held = jnp.where(gone, -1, held)
    sourced = lax.dynamic_slice_in_dim(spill_slots, me * per_rank, per_rank, 0)
    targets = jnp.concatenate([held, sourced])
    columns = jnp.arange(block_table.shape[1], dtype=jnp.int32)[None, :, None]
    match = block_table[:, :, None] == targets[None, None, :]
    limits = jnp.sum(jnp.where(match, context_lengths[:, None, None] - columns * tokens + FAR, 0), axis=1) - FAR

    q = queries.reshape(rows_here, KV, GROUPS, HEAD).transpose(1, 2, 0, 3).reshape(KV, GROUPS * rows_here, HEAD)
    q = jnp.pad(q, ((0, 0), (0, ROWS - GROUPS * rows_here), (0, 0)))

    bf, f32 = jnp.bfloat16, jnp.float32
    vmem = pltpu.VMEM
    dma = pltpu.SemaphoreType.DMA
    any_spec = pl.BlockSpec(memory_space=pl.ANY)
    smem_spec = pl.BlockSpec(memory_space=pltpu.SMEM)
    vmem_spec = pl.BlockSpec(memory_space=pltpu.VMEM)
    block = (tokens, width)
    att, newk, newv = pl.pallas_call(
        functools.partial(exchange_kernel, chips, lanes),
        out_shape=(
            jax.ShapeDtypeStruct((KV, ROWS, HEAD), bf),
            jax.ShapeDtypeStruct((per_rank, *block), bf),
            jax.ShapeDtypeStruct((per_rank, *block), bf),
        ),
        in_specs=[smem_spec, smem_spec, vmem_spec] + [any_spec] * 4,
        out_specs=(vmem_spec, any_spec, any_spec),
        scratch_shapes=[
            vmem((blocks, *block), bf),
            vmem((blocks, *block), bf),
            vmem((chip_blocks, *block), bf),
            vmem((2, lanes, *block), bf),
            vmem((2, lanes, *block), bf),
            vmem((per_rank, *block), bf),
            vmem((per_rank, *block), bf),
            vmem((per_rank, *block), bf),
            vmem((ranks, KV, ROWS, HEAD), bf),
            vmem((ranks * ROWS, blocks * tokens), f32),
            vmem((ranks, KV, ROWS, HEAD), bf),
            vmem((ranks, ROWS, HEAD), f32),
            vmem((chips, KV, ROWS, HEAD), bf),
            vmem((chips, ROWS, HEAD), f32),
            vmem((chips, KV, ROWS, HEAD), bf),
            vmem((chips, ROWS, HEAD), f32),
            vmem((chips, KV, ROWS, HEAD), bf),
            vmem((chips, ROWS, HEAD), f32),
            pltpu.SMEM((2, lanes), jnp.int32),
            dma((5,)),
            dma,
            dma,
            dma((2 * chips - 1,)),
            dma((ranks,)),
            dma((2, lanes, PIECES)),
            dma((2, lanes, PIECES)),
            dma((2,)),
            dma((2,)),
            dma((2, chips)),
            dma((2, chips)),
            dma,
            dma,
            dma((2,)),
        ],
        compiler_params=pltpu.CompilerParams(
            collective_id=0, has_side_effects=True, vmem_limit_bytes=48 * 1024 * 1024
        ),
        name="exchange",
    )(limits, spill_slots, q, prefill_keys, prefill_values, cache_keys, pool_values_prior)

    pool_keys, pool_values, att = pl.pallas_call(
        place_kernel,
        out_shape=(
            jax.ShapeDtypeStruct(cache_keys.shape, bf),
            jax.ShapeDtypeStruct(cache_keys.shape, bf),
            jax.ShapeDtypeStruct(att.shape, bf),
        ),
        in_specs=[smem_spec, smem_spec] + [any_spec] * 5,
        out_specs=(any_spec,) * 3,
        scratch_shapes=[dma((2, rank_slots)), dma],
        name="place",
    )(spill_slots, first.reshape(1), cache_keys, pool_values_prior, newk, newv, att)
    attended = att[:, : GROUPS * rows_here].reshape(KV, GROUPS, rows_here, HEAD).transpose(2, 0, 1, 3)
    return attended.reshape(rows_here, query_width), pool_keys, pool_values


def solution(mesh):
    both = ("grp", "blk")
    return jax.shard_map(
        per_device,
        mesh=mesh,
        in_specs=(P(both, None),) + (P(both, None, None),) * 4 + (P("grp"), P("grp", None), P("grp")),
        out_specs=(P(both, None), P(both, None, None), P(both, None, None)),
        check_vma=False,
    )
```

```python
import functools

import jax
import jax.numpy as jnp
from jax import lax
from jax.experimental import pallas as pl
from jax.experimental.pallas import tpu as pltpu
from jax.sharding import PartitionSpec as P

QUERY_HEADS = 40
KV = 8
GROUPS = QUERY_HEADS // KV
HEAD = 128
STEPS = 4
REQ = 4
ROWS = 16
PIECES = 4
HEADS_PER_STEP = 2
LOW = -1e30
FAR = 1 << 24
VMEM_BYTES = 60 * 1024 * 1024
MESH = pl.DeviceIdType.MESH


def lane_plan(spill, chips, z, lanes, chip_blocks, rank_slots):
    total = chips * chip_blocks
    rank_of = [spill[b] // rank_slots for b in range(total)]
    chip_of = [r // 2 for r in rank_of]
    sends, arrivals = [], []
    for way in range(2):
        dest = chip_of if way == 0 else [chips - 1 - c for c in chip_of]
        place = z if way == 0 else chips - 1 - z
        lane_dest = [jnp.int32(-1)] * lanes
        lane_block = [jnp.int32(-1)] * lanes
        send = [jnp.int32(chip_blocks)] * lanes
        arrive = [jnp.int32(-1)] * lanes
        for n in range(chips):
            here = place == n
            if n > 0:
                arrive = [jnp.where(here, lane_block[l], arrive[l]) for l in range(lanes)]
            if n == chips - 1:
                break
            first = (n if way == 0 else chips - 1 - n) * chip_blocks
            left = [dest[first + i] > n for i in range(chip_blocks)]
            for l in reversed(range(min(lanes, chip_blocks * (n + 1)))):
                pick, pick_dest = jnp.int32(chip_blocks), jnp.int32(-1)
                for i in reversed(range(chip_blocks)):
                    pick = jnp.where(left[i], i, pick)
                    pick_dest = jnp.where(left[i], dest[first + i], pick_dest)
                take = (lane_dest[l] <= n) & (pick < chip_blocks)
                left = [left[i] & jnp.logical_not(take & (pick == i)) for i in range(chip_blocks)]
                lane_dest[l] = jnp.where(take, pick_dest, lane_dest[l])
                lane_block[l] = jnp.where(take, first + pick, lane_block[l])
                send[l] = jnp.where(here & take, pick, send[l])
        sends.append(send)
        arrivals.append(arrive)
    return rank_of, sends, arrivals


def blocks_for(rank, rank_of, per_rank):
    found = [jnp.int32(0)] * per_rank
    count = jnp.int32(0)
    for b, target in enumerate(rank_of):
        hit = target == rank
        found = [jnp.where(hit & (count == q), b, found[q]) for q in range(per_rank)]
        count = count + hit.astype(jnp.int32)
    return found


def exchange_kernel(
    chips, lanes, lengths, table, spill, q_in, pk, pv, ck, cv,
    att, newk, newv,
    kall, vall, own, arr, snd, fin, pout, pin, qg, bias, part, lse, pin_o, pin_l, mo, ml, ro, rl, sched, q_wide, q_ref, att_wide,
    loc, ex_s, ex_r, q_s, q_r, lane_s, lane_r, s1_s, s1_r, s2_s, s2_r, fx_s, fx_r, out_s,
):
    rank_slots, tokens, width = ck.shape
    per_rank = pk.shape[0]
    chip_blocks = 2 * per_rank
    blocks = rank_slots + per_rank
    rows_here = STEPS * REQ // (2 * chips)
    piece = tokens // PIECES
    me = lax.axis_index("blk")
    z = me // 2
    core = lax.rem(me, 2)
    partner = 2 * z + 1 - core

    def remote(src, dst, s, r, rank):
        return pltpu.make_async_remote_copy(
            src_ref=src, dst_ref=dst, send_sem=s, recv_sem=r, device_id={"blk": rank}, device_id_type=MESH
        )

    load_kp = pltpu.make_async_copy(pk, kall.at[pl.ds(rank_slots, per_rank)], loc.at[0])
    load_vp = pltpu.make_async_copy(pv, vall.at[pl.ds(rank_slots, per_rank)], loc.at[1])
    load_kc = pltpu.make_async_copy(ck, kall.at[pl.ds(0, rank_slots)], loc.at[2])
    load_vc = pltpu.make_async_copy(cv, vall.at[pl.ds(0, rank_slots)], loc.at[3])
    own_mine = own.at[pl.ds(core * per_rank, per_rank)]

    @pl.when(core == 0)
    def _():
        pltpu.make_async_copy(pk, own_mine, loc.at[4]).start()

    @pl.when(core == 1)
    def _():
        pltpu.make_async_copy(pv, own_mine, loc.at[4]).start()

    load_kp.start()
    load_vp.start()
    load_kc.start()
    load_vc.start()

    barrier = pltpu.get_barrier_semaphore()
    pl.semaphore_signal(barrier, inc=1, device_id={"blk": partner}, device_id_type=MESH)
    for off in range(1, chips):
        peer = 2 * lax.rem(z + off, chips) + core
        pl.semaphore_signal(barrier, inc=1, device_id={"blk": peer}, device_id_type=MESH)
    pl.semaphore_wait(barrier, chips)

    @pl.when(core == 0)
    def _():
        remote(pv, own_mine, ex_s, ex_r, partner).start()

    @pl.when(core == 1)
    def _():
        remote(pk, own_mine, ex_s, ex_r, partner).start()

    mine = core * chips + z
    q_wide[...] = jnp.zeros_like(q_wide)
    q_rows = q_in[...].astype(jnp.float32)
    for h in range(KV):
        for j in range(GROUPS * rows_here):
            head = h * GROUPS + j // rows_here
            i = j % rows_here
            q_wide[h, j : j + 1, :] = q_rows[i : i + 1, head * HEAD : (head + 1) * HEAD]
    q_ref[...] = q_wide[...].astype(jnp.bfloat16)
    q_copies = [remote(q_ref, qg.at[mine], q_s.at[0], q_r.at[mine], partner)]
    for off in range(1, chips):
        peer = 2 * lax.rem(z + off, chips) + core
        q_copies.append(remote(q_ref, qg.at[mine], q_s.at[off], q_r.at[mine], peer))
    for copy in q_copies:
        copy.start()
    qg[mine] = q_ref[...]

    rank_of, sends, arrivals = lane_plan(spill, chips, z, lanes, chip_blocks, rank_slots)
    for way in range(2):
        for l in range(lanes):
            sched[way, l] = sends[way][l]

    pltpu.make_async_copy(pk, own_mine, loc.at[4]).wait()
    own_other = own.at[pl.ds((1 - core) * per_rank, per_rank)]
    arrived = remote(pk, own_other, ex_s, ex_r, partner)
    arrived.wait_recv()

    low_half = z < chips // 2
    near = jnp.where(low_half, z, chips - 1 - z)
    far = chips - 1 - near
    near_way = jnp.where(low_half, 0, 1)
    far_way = 1 - near_way
    near_next = 2 * jnp.where(low_half, z + 1, z - 1) + core
    far_next = 2 * jnp.where(low_half, jnp.maximum(z - 1, 0), jnp.minimum(z + 1, chips - 1)) + core

    def lane_copy(way, l, p, rank):
        rows = pl.ds(p * piece, piece)
        return remote(
            snd.at[way, l, rows], arr.at[way, l, rows], lane_s.at[way, l, p], lane_r.at[way, l, p], rank
        )

    def compose(way, l, p):
        rows = pl.ds(p * piece, piece)
        pick = sched[way, l]
        snd[way, l, rows] = lax.select(
            pick == chip_blocks, arr[way, l, rows], own[jnp.minimum(pick, chip_blocks - 1), rows]
        )

    def compose_own(way, l, p):
        rows = pl.ds(p * piece, piece)
        snd[way, l, rows] = own[jnp.minimum(sched[way, l], chip_blocks - 1), rows]

    def near_step(i):
        l = lanes - 1 - i
        passing = l < chip_blocks * near
        starting = jnp.logical_not(passing) & (l < chip_blocks * (near + 1))

        @pl.when((l + 2 < lanes) & (l + 2 < chip_blocks * (near + 1)))
        def _():
            for p in range(PIECES):
                lane_copy(near_way, l + 2, p, near_next).wait_send()

        @pl.when(passing)
        def _():
            for p in range(PIECES):
                lane_copy(near_way, l, p, near_next).wait_recv()
                compose(near_way, l, p)
                lane_copy(near_way, l, p, near_next).start()

        @pl.when(starting)
        def _():
            for p in range(PIECES):
                compose_own(near_way, l, p)
                lane_copy(near_way, l, p, near_next).start()

    def far_step(i):
        l = lanes - 1 - i

        @pl.when(far < chips - 1)
        def _():
            for p in range(PIECES):
                lane_copy(far_way, l, p, far_next).wait_recv()
                compose(far_way, l, p)
                lane_copy(far_way, l, p, far_next).start()

    def attend(h):
        cols = pl.ds(pl.multiple_of(h * HEAD, HEAD), HEAD)
        q = qg[:, h].reshape(2 * chips * ROWS, HEAD)
        k = kall[:, :, cols].reshape(blocks * tokens, HEAD)
        v = vall[:, :, cols].reshape(blocks * tokens, HEAD)
        s = lax.dot_general(q, k, (((1,), (1,)), ((), ())), preferred_element_type=jnp.float32)
        s = s * HEAD ** (-0.5) + bias[...]
        m = jnp.max(s, axis=1, keepdims=True)
        w = jnp.exp(s - m)
        total = jnp.sum(w, axis=1, keepdims=True)
        o = jnp.dot(w.astype(jnp.bfloat16), v, preferred_element_type=jnp.float32) / total
        part[:, h] = o.reshape(2 * chips, ROWS, HEAD)
        lane = lax.broadcasted_iota(jnp.int32, (2 * chips, ROWS, HEAD), 2)
        level = (m + jnp.log(total)).reshape(2 * chips, ROWS, 1)
        lse[...] = jnp.where(lane == h, level, lse[...])

    near_step(0)

    for off in range(1, chips):
        other = core * chips + lax.rem(z + off, chips)
        remote(q_ref, qg.at[other], q_s.at[0], q_r.at[other], partner).wait_recv()
        remote(qg.at[other], qg.at[other], q_s.at[chips - 1 + off], q_r.at[other], partner).start()

    row_count = 2 * chips * ROWS
    row = lax.broadcasted_iota(jnp.int32, (row_count, HEAD), 0)
    slot, inner = row // ROWS, row % ROWS
    rank_row = 2 * (slot % chips) + slot // chips
    row_id = rank_row * rows_here + inner % rows_here
    valid = inner < GROUPS * rows_here
    step, request = row_id // REQ, row_id % REQ
    token = lax.broadcasted_iota(jnp.int32, (row_count, HEAD), 1)
    edge = jnp.where(valid, token + (STEPS - 1) - step, FAR).astype(jnp.float32)
    columns = table.shape[1]
    owned = jnp.broadcast_to(table[0:1, :], (row_count, columns))
    length = jnp.full((row_count, columns), lengths[0], jnp.int32)
    for r in range(1, REQ):
        here = request[:, :columns] == r
        owned = jnp.where(here, table[r : r + 1, :], owned)
        length = jnp.where(here, lengths[r], length)
    after = (length - lax.broadcasted_iota(jnp.int32, (row_count, columns), 1) * tokens).astype(jnp.float32)
    for s in range(blocks):
        if s < rank_slots:
            block_id = me * rank_slots + s
            for b in range(chips * chip_blocks):
                block_id = jnp.where(spill[b] == me * rank_slots + s, -1, block_id)
        else:
            block_id = spill[me * per_rank + s - rank_slots]
        bound = jnp.max(jnp.where(owned == block_id, after, float(-FAR)), axis=1, keepdims=True)
        bias[:, pl.ds(s * tokens, tokens)] = jnp.where(edge < bound, 0.0, LOW).astype(jnp.float32)
    lse[...] = jnp.zeros_like(lse)

    load_kp.wait()
    load_vp.wait()
    load_kc.wait()
    load_vc.wait()
    for zz in range(chips):
        other = (1 - core) * chips + zz
        remote(q_ref, qg.at[other], q_s.at[0], q_r.at[other], partner).wait_recv()

    attending = KV // HEADS_PER_STEP

    def mixed(i, carry):
        near_step(i)
        far_step(i - 1)
        for e in range(HEADS_PER_STEP):
            attend((i - 1) * HEADS_PER_STEP + e)
        return carry

    lax.fori_loop(1, 1 + attending, mixed, 0)

    theirs = pl.ds((1 - core) * chips, chips)
    s1_o = remote(part.at[theirs], pin_o, s1_s.at[0], s1_r.at[0], partner)
    s1_l = remote(lse.at[theirs], pin_l, s1_s.at[1], s1_r.at[1], partner)
    s1_o.start()
    s1_l.start()
    near_step(1 + attending)
    far_step(attending)
    s1_o.wait_recv()
    s1_l.wait_recv()

    ours = pl.ds(core * chips, chips)
    level_a, level_b = lse[ours], pin_l[...]
    top = jnp.maximum(level_a, level_b)
    ea, eb = jnp.exp(level_a - top), jnp.exp(level_b - top)
    both = ea + eb
    ml[...] = top + jnp.log(both)
    wa, wb = ea / both, eb / both
    for h in range(KV):
        mixed_rows = part[ours, h] * wa[:, :, h : h + 1] + pin_o[:, h] * wb[:, :, h : h + 1]
        mo[:, h] = mixed_rows.astype(jnp.bfloat16)
    s2 = []
    for off in range(1, chips):
        to = lax.rem(z + off, chips)
        s2.append(remote(mo.at[to], ro.at[z], s2_s.at[0, off], s2_r.at[0, z], 2 * to + core))
        s2.append(remote(ml.at[to], rl.at[z], s2_s.at[1, off], s2_r.at[1, z], 2 * to + core))
    for copy in s2:
        copy.start()
    ro[z] = mo[z]
    rl[z] = ml[z]

    def moving(i, carry):
        near_step(i)
        far_step(i - 1)
        return carry

    lax.fori_loop(2 + attending, lanes, moving, 0)
    far_step(lanes - 1)

    for off in range(1, chips):
        source = lax.rem(z + off, chips)
        remote(mo.at[source], ro.at[source], s2_s.at[0, off], s2_r.at[0, source], partner).wait_recv()
        remote(ml.at[source], rl.at[source], s2_s.at[1, off], s2_r.at[1, source], partner).wait_recv()
    levels = rl[...]
    top = jnp.max(levels, axis=0, keepdims=True)
    shares = jnp.exp(levels - top)
    shares = shares / jnp.sum(shares, axis=0, keepdims=True)
    for h in range(KV):
        rows = jnp.sum(ro[:, h].astype(jnp.float32) * shares[:, :, h : h + 1], axis=0)
        for j in range(GROUPS * rows_here):
            head = h * GROUPS + j // rows_here
            i = j % rows_here
            att_wide[i : i + 1, head * HEAD : (head + 1) * HEAD] = rows[j : j + 1, :]
    att[...] = att_wide[...].astype(jnp.bfloat16)

    @pl.when(far == chips - 1)
    def _():
        def drain(i, carry):
            for p in range(PIECES):
                lane_copy(far_way, lanes - 1 - i, p, far_next).wait_recv()
            return carry

        lax.fori_loop(0, lanes, drain, 0)

    def gathered(b, q, target):
        at_home = b // chip_blocks == z
        index = jnp.clip(b - z * chip_blocks, 0, chip_blocks - 1)
        way_of, lane_of = jnp.int32(0), jnp.int32(0)
        for way in range(2):
            for l in range(lanes):
                hit = arrivals[way][l] == b
                way_of = jnp.where(hit, way, way_of)
                lane_of = jnp.where(hit, l, lane_of)
        target[q] = lax.select(at_home, own[index], arr[way_of, lane_of])

    for q, b in enumerate(blocks_for(partner, rank_of, per_rank)):
        gathered(b, q, pout)
    handed = remote(pout, pin, fx_s, fx_r, partner)
    handed.start()
    for q, b in enumerate(blocks_for(me, rank_of, per_rank)):
        gathered(b, q, fin)

    @pl.when(core == 0)
    def _():
        pltpu.make_async_copy(fin, newk, out_s.at[0]).start()

    @pl.when(core == 1)
    def _():
        pltpu.make_async_copy(fin, newv, out_s.at[0]).start()

    handed.wait_recv()

    @pl.when(core == 0)
    def _():
        pltpu.make_async_copy(pin, newv, out_s.at[1]).start()

    @pl.when(core == 1)
    def _():
        pltpu.make_async_copy(pin, newk, out_s.at[1]).start()

    handed.wait_send()
    arrived.wait_send()
    s1_o.wait_send()
    s1_l.wait_send()
    for copy in s2:
        copy.wait_send()
    for off in range(2 * chips - 1):
        remote(q_ref, qg.at[mine], q_s.at[off], q_r.at[mine], partner).wait_send()
    for l in range(2):
        @pl.when(l < chip_blocks * (near + 1))
        def _():
            for p in range(PIECES):
                lane_copy(near_way, l, p, near_next).wait_send()

    @pl.when(far < chips - 1)
    def _():
        def sent(i, carry):
            for p in range(PIECES):
                lane_copy(far_way, i, p, far_next).wait_send()
            return carry

        lax.fori_loop(0, lanes, sent, 0)

    pltpu.make_async_copy(fin, newk, out_s.at[0]).wait()
    pltpu.make_async_copy(pin, newv, out_s.at[1]).wait()


def place_kernel(spill, first_ref, ck, cv, newk, newv, att_in, pool_k, pool_v, att_out, hold, into, out):
    rank_slots = ck.shape[0]
    first = first_ref[0]
    filled = [jnp.bool_(False)] * rank_slots
    count = jnp.int32(0)
    for b in range(spill.shape[0]):
        at = spill[b] - first
        mine = (at >= 0) & (at < rank_slots)
        filled = [filled[j] | (at == j) for j in range(rank_slots)]
        here, which = jnp.clip(at, 0, rank_slots - 1), jnp.minimum(count, newk.shape[0] - 1)

        @pl.when(mine)
        def _():
            pltpu.make_async_copy(newk.at[which], hold.at[0, here], into.at[0, here]).start()
            pltpu.make_async_copy(newv.at[which], hold.at[1, here], into.at[1, here]).start()

        count = count + mine.astype(jnp.int32)
    for j in range(rank_slots):
        @pl.when(jnp.logical_not(filled[j]))
        def _():
            pltpu.make_async_copy(ck.at[j], hold.at[0, j], into.at[0, j]).start()
            pltpu.make_async_copy(cv.at[j], hold.at[1, j], into.at[1, j]).start()

    att_out[...] = att_in[...]
    stores = []
    for j in range(rank_slots):
        for t, (source, target) in enumerate(((ck, pool_k), (cv, pool_v))):
            pltpu.make_async_copy(source.at[j], hold.at[t, j], into.at[t, j]).wait()
            stores.append(pltpu.make_async_copy(hold.at[t, j], target.at[j], out.at[t, j]))
            stores[-1].start()
    for copy in stores:
        copy.wait()


def per_device(
    queries, cache_keys, pool_values_prior, prefill_keys, prefill_values, context_lengths, block_table, spill_slots
):
    ranks = lax.axis_size("blk")
    chips = ranks // 2
    me = lax.axis_index("blk")
    rank_slots, tokens, width = cache_keys.shape
    per_rank = prefill_keys.shape[0]
    chip_blocks = 2 * per_rank
    blocks = rank_slots + per_rank
    lanes = chip_blocks * (chips // 2)
    rows_here, query_width = queries.shape
    first = me * rank_slots

    bf, f32 = jnp.bfloat16, jnp.float32
    vmem = pltpu.VMEM
    dma = pltpu.SemaphoreType.DMA
    any_spec = pl.BlockSpec(memory_space=pl.ANY)
    smem_spec = pl.BlockSpec(memory_space=pltpu.SMEM)
    vmem_spec = pl.BlockSpec(memory_space=pltpu.VMEM)
    block = (tokens, width)
    att, newk, newv = pl.pallas_call(
        functools.partial(exchange_kernel, chips, lanes),
        out_shape=(
            jax.ShapeDtypeStruct(queries.shape, bf),
            jax.ShapeDtypeStruct((per_rank, *block), bf),
            jax.ShapeDtypeStruct((per_rank, *block), bf),
        ),
        in_specs=[smem_spec, vmem_spec, smem_spec, vmem_spec] + [any_spec] * 4,
        out_specs=(vmem_spec, any_spec, any_spec),
        scratch_shapes=[
            vmem((blocks, *block), bf),
            vmem((blocks, *block), bf),
            vmem((chip_blocks, *block), bf),
            vmem((2, lanes, *block), bf),
            vmem((2, lanes, *block), bf),
            vmem((per_rank, *block), bf),
            vmem((per_rank, *block), bf),
            vmem((per_rank, *block), bf),
            vmem((ranks, KV, ROWS, HEAD), bf),
            vmem((ranks * ROWS, blocks * tokens), f32),
            vmem((ranks, KV, ROWS, HEAD), f32),
            vmem((ranks, ROWS, HEAD), f32),
            vmem((chips, KV, ROWS, HEAD), f32),
            vmem((chips, ROWS, HEAD), f32),
            vmem((chips, KV, ROWS, HEAD), bf),
            vmem((chips, ROWS, HEAD), f32),
            vmem((chips, KV, ROWS, HEAD), bf),
            vmem((chips, ROWS, HEAD), f32),
            pltpu.SMEM((2, lanes), jnp.int32),
            vmem((KV, ROWS, HEAD), f32),
            vmem((KV, ROWS, HEAD), bf),
            vmem(queries.shape, f32),
            dma((5,)),
            dma,
            dma,
            dma((2 * chips - 1,)),
            dma((ranks,)),
            dma((2, lanes, PIECES)),
            dma((2, lanes, PIECES)),
            dma((2,)),
            dma((2,)),
            dma((2, chips)),
            dma((2, chips)),
            dma,
            dma,
            dma((2,)),
        ],
        compiler_params=pltpu.CompilerParams(
            collective_id=0, has_side_effects=True, vmem_limit_bytes=VMEM_BYTES
        ),
        name="exchange",
    )(context_lengths, block_table, spill_slots, queries, prefill_keys, prefill_values, cache_keys, pool_values_prior)

    pool_keys, pool_values, att = pl.pallas_call(
        place_kernel,
        out_shape=(
            jax.ShapeDtypeStruct(cache_keys.shape, bf),
            jax.ShapeDtypeStruct(cache_keys.shape, bf),
            jax.ShapeDtypeStruct(att.shape, bf),
        ),
        in_specs=[smem_spec, smem_spec] + [any_spec] * 4 + [vmem_spec],
        out_specs=(any_spec, any_spec, vmem_spec),
        scratch_shapes=[vmem((2, rank_slots, *block), bf), dma((2, rank_slots)), dma((2, rank_slots))],
        compiler_params=pltpu.CompilerParams(vmem_limit_bytes=VMEM_BYTES),
        name="place",
    )(spill_slots, first.reshape(1), cache_keys, pool_values_prior, newk, newv, att)
    return att, pool_keys, pool_values


def solution(mesh):
    both = ("grp", "blk")
    return jax.shard_map(
        per_device,
        mesh=mesh,
        in_specs=(P(both, None),) + (P(both, None, None),) * 4 + (P("grp"), P("grp", None), P("grp")),
        out_specs=(P(both, None), P(both, None, None), P(both, None, None)),
        check_vma=False,
    )
```

```python
import functools

import jax
import jax.numpy as jnp
from jax import lax
from jax.experimental import pallas as pl
from jax.experimental.pallas import tpu as pltpu
from jax.sharding import PartitionSpec as P

QUERY_HEADS = 40
KV = 8
GROUPS = QUERY_HEADS // KV
HEAD = 128
STEPS = 4
REQ = 4
ROWS = 16
PIECES = 4
HEADS_PER_STEP = 2
LOW = -1e30
FAR = 1 << 24
VMEM_BYTES = 60 * 1024 * 1024
MESH = pl.DeviceIdType.MESH


def lane_plan(spill, chips, z, lanes, chip_blocks, rank_slots):
    total = chips * chip_blocks
    rank_of = [spill[b] // rank_slots for b in range(total)]
    chip_of = [r // 2 for r in rank_of]
    sends, arrivals = [], []
    for way in range(2):
        dest = chip_of if way == 0 else [chips - 1 - c for c in chip_of]
        place = z if way == 0 else chips - 1 - z
        lane_dest = [jnp.int32(-1)] * lanes
        lane_block = [jnp.int32(-1)] * lanes
        send = [jnp.int32(chip_blocks)] * lanes
        arrive = [jnp.int32(-1)] * lanes
        for n in range(chips):
            here = place == n
            if n > 0:
                arrive = [jnp.where(here, lane_block[l], arrive[l]) for l in range(lanes)]
            if n == chips - 1:
                break
            first = (n if way == 0 else chips - 1 - n) * chip_blocks
            left = [dest[first + i] > n for i in range(chip_blocks)]
            for l in reversed(range(min(lanes, chip_blocks * (n + 1)))):
                pick, pick_dest = jnp.int32(chip_blocks), jnp.int32(-1)
                for i in reversed(range(chip_blocks)):
                    pick = jnp.where(left[i], i, pick)
                    pick_dest = jnp.where(left[i], dest[first + i], pick_dest)
                take = (lane_dest[l] <= n) & (pick < chip_blocks)
                left = [left[i] & jnp.logical_not(take & (pick == i)) for i in range(chip_blocks)]
                lane_dest[l] = jnp.where(take, pick_dest, lane_dest[l])
                lane_block[l] = jnp.where(take, first + pick, lane_block[l])
                send[l] = jnp.where(here & take, pick, send[l])
        sends.append(send)
        arrivals.append(arrive)
    return rank_of, sends, arrivals


def blocks_for(rank, rank_of, per_rank):
    found = [jnp.int32(0)] * per_rank
    count = jnp.int32(0)
    for b, target in enumerate(rank_of):
        hit = target == rank
        found = [jnp.where(hit & (count == q), b, found[q]) for q in range(per_rank)]
        count = count + hit.astype(jnp.int32)
    return found


def exchange_kernel(
    chips, lanes, lengths, table, spill, q_in, pk, pv, ck, cv,
    att, newk, newv,
    kall, vall, own, arr, snd, fin, pout, pin, qg, bias, part, lse, pin_o, pin_l, mo, ml, ro, rl, sched, q_wide, q_ref, att_wide,
    loc, ex_s, ex_r, q_s, q_r, lane_s, lane_r, s1_s, s1_r, s2_s, s2_r, fx_s, fx_r, out_s,
):
    rank_slots, tokens, width = ck.shape
    per_rank = pk.shape[0]
    chip_blocks = 2 * per_rank
    blocks = rank_slots + per_rank
    rows_here = STEPS * REQ // (2 * chips)
    piece = tokens // PIECES
    me = lax.axis_index("blk")
    z = me // 2
    core = lax.rem(me, 2)
    partner = 2 * z + 1 - core

    def remote(src, dst, s, r, rank):
        return pltpu.make_async_remote_copy(
            src_ref=src, dst_ref=dst, send_sem=s, recv_sem=r, device_id={"blk": rank}, device_id_type=MESH
        )

    load_kp = pltpu.make_async_copy(pk, kall.at[pl.ds(rank_slots, per_rank)], loc.at[0])
    load_vp = pltpu.make_async_copy(pv, vall.at[pl.ds(rank_slots, per_rank)], loc.at[1])
    load_kc = pltpu.make_async_copy(ck, kall.at[pl.ds(0, rank_slots)], loc.at[2])
    load_vc = pltpu.make_async_copy(cv, vall.at[pl.ds(0, rank_slots)], loc.at[3])
    own_mine = own.at[pl.ds(core * per_rank, per_rank)]

    @pl.when(core == 0)
    def _():
        pltpu.make_async_copy(pk, own_mine, loc.at[4]).start()

    @pl.when(core == 1)
    def _():
        pltpu.make_async_copy(pv, own_mine, loc.at[4]).start()

    load_kp.start()
    load_vp.start()
    load_kc.start()
    load_vc.start()

    barrier = pltpu.get_barrier_semaphore()
    pl.semaphore_signal(barrier, inc=1, device_id={"blk": partner}, device_id_type=MESH)
    for off in range(1, chips):
        peer = 2 * lax.rem(z + off, chips) + core
        pl.semaphore_signal(barrier, inc=1, device_id={"blk": peer}, device_id_type=MESH)
    pl.semaphore_wait(barrier, chips)

    @pl.when(core == 0)
    def _():
        remote(pv, own_mine, ex_s, ex_r, partner).start()

    @pl.when(core == 1)
    def _():
        remote(pk, own_mine, ex_s, ex_r, partner).start()

    mine = core * chips + z
    q_wide[...] = jnp.zeros_like(q_wide)
    q_rows = q_in[...].astype(jnp.float32)
    for h in range(KV):
        for j in range(GROUPS * rows_here):
            head = h * GROUPS + j // rows_here
            i = j % rows_here
            q_wide[h, j : j + 1, :] = q_rows[i : i + 1, head * HEAD : (head + 1) * HEAD]
    q_ref[...] = q_wide[...].astype(jnp.bfloat16)
    q_copies = [remote(q_ref, qg.at[mine], q_s.at[0], q_r.at[mine], partner)]
    for off in range(1, chips):
        peer = 2 * lax.rem(z + off, chips) + core
        q_copies.append(remote(q_ref, qg.at[mine], q_s.at[off], q_r.at[mine], peer))
    for copy in q_copies:
        copy.start()
    qg[mine] = q_ref[...]

    rank_of, sends, arrivals = lane_plan(spill, chips, z, lanes, chip_blocks, rank_slots)
    for way in range(2):
        for l in range(lanes):
            sched[way, l] = sends[way][l]

    pltpu.make_async_copy(pk, own_mine, loc.at[4]).wait()
    own_other = own.at[pl.ds((1 - core) * per_rank, per_rank)]
    arrived = remote(pk, own_other, ex_s, ex_r, partner)
    arrived.wait_recv()

    low_half = z < chips // 2
    near = jnp.where(low_half, z, chips - 1 - z)
    far = chips - 1 - near
    near_way = jnp.where(low_half, 0, 1)
    far_way = 1 - near_way
    near_next = 2 * jnp.where(low_half, z + 1, z - 1) + core
    far_next = 2 * jnp.where(low_half, jnp.maximum(z - 1, 0), jnp.minimum(z + 1, chips - 1)) + core

    def lane_copy(way, l, p, rank):
        rows = pl.ds(p * piece, piece)
        return remote(
            snd.at[way, l, rows], arr.at[way, l, rows], lane_s.at[way, l, p], lane_r.at[way, l, p], rank
        )

    def compose(way, l, p):
        rows = pl.ds(p * piece, piece)
        pick = sched[way, l]
        snd[way, l, rows] = lax.select(
            pick == chip_blocks, arr[way, l, rows], own[jnp.minimum(pick, chip_blocks - 1), rows]
        )

    def compose_own(way, l, p):
        rows = pl.ds(p * piece, piece)
        snd[way, l, rows] = own[jnp.minimum(sched[way, l], chip_blocks - 1), rows]

    def near_step(i):
        l = lanes - 1 - i
        if isinstance(i, int) and l < 0:
            return
        passing = (l >= 0) & (l < chip_blocks * near)
        starting = (l >= 0) & jnp.logical_not(passing) & (l < chip_blocks * (near + 1))

        @pl.when((l >= 0) & (l + 2 < lanes) & (l + 2 < chip_blocks * (near + 1)))
        def _():
            for p in range(PIECES):
                lane_copy(near_way, l + 2, p, near_next).wait_send()

        @pl.when(passing)
        def _():
            for p in range(PIECES):
                lane_copy(near_way, l, p, near_next).wait_recv()
                compose(near_way, l, p)
                lane_copy(near_way, l, p, near_next).start()

        @pl.when(starting)
        def _():
            for p in range(PIECES):
                compose_own(near_way, l, p)
                lane_copy(near_way, l, p, near_next).start()

    def far_step(i):
        l = lanes - 1 - i
        if isinstance(i, int) and l < 0:
            return

        @pl.when((l >= 0) & (far < chips - 1))
        def _():
            for p in range(PIECES):
                lane_copy(far_way, l, p, far_next).wait_recv()
                compose(far_way, l, p)
                lane_copy(far_way, l, p, far_next).start()

    def attend(h):
        cols = pl.ds(pl.multiple_of(h * HEAD, HEAD), HEAD)
        q = qg[:, h].reshape(2 * chips * ROWS, HEAD)
        k = kall[:, :, cols].reshape(blocks * tokens, HEAD)
        v = vall[:, :, cols].reshape(blocks * tokens, HEAD)
        s = lax.dot_general(q, k, (((1,), (1,)), ((), ())), preferred_element_type=jnp.float32)
        s = s * HEAD ** (-0.5) + bias[...]
        m = jnp.max(s, axis=1, keepdims=True)
        w = jnp.exp(s - m)
        total = jnp.sum(w, axis=1, keepdims=True)
        o = jnp.dot(w.astype(jnp.bfloat16), v, preferred_element_type=jnp.float32) / total
        part[:, h] = o.reshape(2 * chips, ROWS, HEAD)
        lane = lax.broadcasted_iota(jnp.int32, (2 * chips, ROWS, HEAD), 2)
        level = (m + jnp.log(total)).reshape(2 * chips, ROWS, 1)
        lse[...] = jnp.where(lane == h, level, lse[...])

    near_step(0)

    for off in range(1, chips):
        other = core * chips + lax.rem(z + off, chips)
        remote(q_ref, qg.at[other], q_s.at[0], q_r.at[other], partner).wait_recv()
        remote(qg.at[other], qg.at[other], q_s.at[chips - 1 + off], q_r.at[other], partner).start()

    row_count = 2 * chips * ROWS
    row = lax.broadcasted_iota(jnp.int32, (row_count, HEAD), 0)
    slot, inner = row // ROWS, row % ROWS
    rank_row = 2 * (slot % chips) + slot // chips
    row_id = rank_row * rows_here + inner % rows_here
    valid = inner < GROUPS * rows_here
    step, request = row_id // REQ, row_id % REQ
    token = lax.broadcasted_iota(jnp.int32, (row_count, HEAD), 1)
    edge = jnp.where(valid, token + (STEPS - 1) - step, FAR).astype(jnp.float32)
    columns = table.shape[1]
    owned = jnp.broadcast_to(table[0:1, :], (row_count, columns))
    length = jnp.full((row_count, columns), lengths[0], jnp.int32)
    for r in range(1, REQ):
        here = request[:, :columns] == r
        owned = jnp.where(here, table[r : r + 1, :], owned)
        length = jnp.where(here, lengths[r], length)
    after = (length - lax.broadcasted_iota(jnp.int32, (row_count, columns), 1) * tokens).astype(jnp.float32)
    for s in range(blocks):
        if s < rank_slots:
            block_id = me * rank_slots + s
            for b in range(chips * chip_blocks):
                block_id = jnp.where(spill[b] == me * rank_slots + s, -1, block_id)
        else:
            block_id = spill[me * per_rank + s - rank_slots]
        bound = jnp.max(jnp.where(owned == block_id, after, float(-FAR)), axis=1, keepdims=True)
        bias[:, pl.ds(s * tokens, tokens)] = jnp.where(edge < bound, 0.0, LOW).astype(jnp.float32)
    lse[...] = jnp.zeros_like(lse)

    load_kp.wait()
    load_vp.wait()
    load_kc.wait()
    load_vc.wait()
    for zz in range(chips):
        other = (1 - core) * chips + zz
        remote(q_ref, qg.at[other], q_s.at[0], q_r.at[other], partner).wait_recv()

    attending = KV // HEADS_PER_STEP

    def mixed(i, carry):
        near_step(i)
        far_step(i - 1)
        for e in range(HEADS_PER_STEP):
            attend((i - 1) * HEADS_PER_STEP + e)
        return carry

    lax.fori_loop(1, 1 + attending, mixed, 0)

    theirs = pl.ds((1 - core) * chips, chips)
    s1_o = remote(part.at[theirs], pin_o, s1_s.at[0], s1_r.at[0], partner)
    s1_l = remote(lse.at[theirs], pin_l, s1_s.at[1], s1_r.at[1], partner)
    s1_o.start()
    s1_l.start()
    near_step(1 + attending)
    far_step(attending)
    s1_o.wait_recv()
    s1_l.wait_recv()

    ours = pl.ds(core * chips, chips)
    level_a, level_b = lse[ours], pin_l[...]
    top = jnp.maximum(level_a, level_b)
    ea, eb = jnp.exp(level_a - top), jnp.exp(level_b - top)
    both = ea + eb
    ml[...] = top + jnp.log(both)
    wa, wb = ea / both, eb / both
    for h in range(KV):
        mixed_rows = part[ours, h] * wa[:, :, h : h + 1] + pin_o[:, h] * wb[:, :, h : h + 1]
        mo[:, h] = mixed_rows.astype(jnp.bfloat16)
    s2 = []
    for off in range(1, chips):
        to = lax.rem(z + off, chips)
        s2.append(remote(mo.at[to], ro.at[z], s2_s.at[0, off], s2_r.at[0, z], 2 * to + core))
        s2.append(remote(ml.at[to], rl.at[z], s2_s.at[1, off], s2_r.at[1, z], 2 * to + core))
    for copy in s2:
        copy.start()
    ro[z] = mo[z]
    rl[z] = ml[z]

    def moving(i, carry):
        near_step(i)
        far_step(i - 1)
        return carry

    if lanes > 2 + attending:
        lax.fori_loop(2 + attending, lanes, moving, 0)
    if lanes > 1 + attending:
        far_step(lanes - 1)

    for off in range(1, chips):
        source = lax.rem(z + off, chips)
        remote(mo.at[source], ro.at[source], s2_s.at[0, off], s2_r.at[0, source], partner).wait_recv()
        remote(ml.at[source], rl.at[source], s2_s.at[1, off], s2_r.at[1, source], partner).wait_recv()
    levels = rl[...]
    top = jnp.max(levels, axis=0, keepdims=True)
    shares = jnp.exp(levels - top)
    shares = shares / jnp.sum(shares, axis=0, keepdims=True)
    for h in range(KV):
        rows = jnp.sum(ro[:, h].astype(jnp.float32) * shares[:, :, h : h + 1], axis=0)
        for j in range(GROUPS * rows_here):
            head = h * GROUPS + j // rows_here
            i = j % rows_here
            att_wide[i : i + 1, head * HEAD : (head + 1) * HEAD] = rows[j : j + 1, :]
    att[...] = att_wide[...].astype(jnp.bfloat16)

    @pl.when(far == chips - 1)
    def _():
        def drain(i, carry):
            for p in range(PIECES):
                lane_copy(far_way, lanes - 1 - i, p, far_next).wait_recv()
            return carry

        lax.fori_loop(0, lanes, drain, 0)

    def gathered(b, q, target):
        at_home = b // chip_blocks == z
        index = jnp.clip(b - z * chip_blocks, 0, chip_blocks - 1)
        way_of, lane_of = jnp.int32(0), jnp.int32(0)
        for way in range(2):
            for l in range(lanes):
                hit = arrivals[way][l] == b
                way_of = jnp.where(hit, way, way_of)
                lane_of = jnp.where(hit, l, lane_of)
        target[q] = lax.select(at_home, own[index], arr[way_of, lane_of])

    for q, b in enumerate(blocks_for(partner, rank_of, per_rank)):
        gathered(b, q, pout)
    handed = remote(pout, pin, fx_s, fx_r, partner)
    handed.start()
    for q, b in enumerate(blocks_for(me, rank_of, per_rank)):
        gathered(b, q, fin)

    @pl.when(core == 0)
    def _():
        pltpu.make_async_copy(fin, newk, out_s.at[0]).start()

    @pl.when(core == 1)
    def _():
        pltpu.make_async_copy(fin, newv, out_s.at[0]).start()

    handed.wait_recv()

    @pl.when(core == 0)
    def _():
        pltpu.make_async_copy(pin, newv, out_s.at[1]).start()

    @pl.when(core == 1)
    def _():
        pltpu.make_async_copy(pin, newk, out_s.at[1]).start()

    handed.wait_send()
    arrived.wait_send()
    s1_o.wait_send()
    s1_l.wait_send()
    for copy in s2:
        copy.wait_send()
    for off in range(2 * chips - 1):
        remote(q_ref, qg.at[mine], q_s.at[off], q_r.at[mine], partner).wait_send()
    for l in range(2):
        @pl.when(l < chip_blocks * (near + 1))
        def _():
            for p in range(PIECES):
                lane_copy(near_way, l, p, near_next).wait_send()

    @pl.when(far < chips - 1)
    def _():
        def sent(i, carry):
            for p in range(PIECES):
                lane_copy(far_way, i, p, far_next).wait_send()
            return carry

        lax.fori_loop(0, lanes, sent, 0)

    pltpu.make_async_copy(fin, newk, out_s.at[0]).wait()
    pltpu.make_async_copy(pin, newv, out_s.at[1]).wait()


def load_kernel(chips, chip_blocks, rank_slots, steps, spill, pick, box, send, recv):
    groups = lax.axis_size("grp")
    mine = lax.axis_index("grp")
    barrier = pltpu.get_barrier_semaphore()
    for off in range(1, groups):
        peer = lax.rem(mine + off, groups)
        pl.semaphore_signal(barrier, inc=1, device_id={"grp": peer}, device_id_type=MESH)
    chip_of = [spill[b] // (2 * rank_slots) for b in range(chips * chip_blocks)]
    load = jnp.int32(0)
    for n in range(chips - 1):
        crossing = jnp.int32(0)
        for b in range((n + 1) * chip_blocks):
            crossing = crossing + (chip_of[b] > n).astype(jnp.int32)
        load = jnp.maximum(load, crossing)
    box[mine] = jnp.full(box.shape[1:], load, jnp.int32)
    pl.semaphore_wait(barrier, groups - 1)

    def copy_to(off, source):
        return pltpu.make_async_remote_copy(
            src_ref=box.at[mine], dst_ref=box.at[mine], send_sem=send.at[off], recv_sem=recv.at[source],
            device_id={"grp": lax.rem(mine + off, groups)}, device_id_type=MESH,
        )

    for off in range(1, groups):
        copy_to(off, mine).start()
    for off in range(1, groups):
        copy_to(off, lax.rem(mine + off, groups)).wait_recv()
    largest = jnp.max(box[...])
    choice = jnp.int32(0)
    for step in steps[:-1]:
        choice = choice + (largest > step).astype(jnp.int32)
    pick[0] = choice
    for off in range(1, groups):
        copy_to(off, mine).wait_send()


def place_kernel(spill, first_ref, ck, cv, newk, newv, att_in, pool_k, pool_v, att_out, hold, into, out):
    rank_slots = ck.shape[0]
    first = first_ref[0]
    filled = [jnp.bool_(False)] * rank_slots
    count = jnp.int32(0)
    for b in range(spill.shape[0]):
        at = spill[b] - first
        mine = (at >= 0) & (at < rank_slots)
        filled = [filled[j] | (at == j) for j in range(rank_slots)]
        here, which = jnp.clip(at, 0, rank_slots - 1), jnp.minimum(count, newk.shape[0] - 1)

        @pl.when(mine)
        def _():
            pltpu.make_async_copy(newk.at[which], hold.at[0, here], into.at[0, here]).start()
            pltpu.make_async_copy(newv.at[which], hold.at[1, here], into.at[1, here]).start()

        count = count + mine.astype(jnp.int32)
    for j in range(rank_slots):
        @pl.when(jnp.logical_not(filled[j]))
        def _():
            pltpu.make_async_copy(ck.at[j], hold.at[0, j], into.at[0, j]).start()
            pltpu.make_async_copy(cv.at[j], hold.at[1, j], into.at[1, j]).start()

    att_out[...] = att_in[...]
    stores = []
    for j in range(rank_slots):
        for t, (source, target) in enumerate(((ck, pool_k), (cv, pool_v))):
            pltpu.make_async_copy(source.at[j], hold.at[t, j], into.at[t, j]).wait()
            stores.append(pltpu.make_async_copy(hold.at[t, j], target.at[j], out.at[t, j]))
            stores[-1].start()
    for copy in stores:
        copy.wait()


def per_device(
    queries, cache_keys, pool_values_prior, prefill_keys, prefill_values, context_lengths, block_table, spill_slots
):
    ranks = lax.axis_size("blk")
    chips = ranks // 2
    me = lax.axis_index("blk")
    rank_slots, tokens, width = cache_keys.shape
    per_rank = prefill_keys.shape[0]
    chip_blocks = 2 * per_rank
    blocks = rank_slots + per_rank
    most = chip_blocks * (chips // 2)
    choices = (most // 2, most * 5 // 8, most * 3 // 4, most)
    rows_here, query_width = queries.shape
    first = me * rank_slots

    bf, f32 = jnp.bfloat16, jnp.float32
    vmem = pltpu.VMEM
    dma = pltpu.SemaphoreType.DMA
    any_spec = pl.BlockSpec(memory_space=pl.ANY)
    smem_spec = pl.BlockSpec(memory_space=pltpu.SMEM)
    vmem_spec = pl.BlockSpec(memory_space=pltpu.VMEM)
    block = (tokens, width)
    def exchange(number, lanes, *operands):
        return pl.pallas_call(
            functools.partial(exchange_kernel, chips, lanes),
            out_shape=(
                jax.ShapeDtypeStruct(queries.shape, bf),
                jax.ShapeDtypeStruct((per_rank, *block), bf),
                jax.ShapeDtypeStruct((per_rank, *block), bf),
            ),
            in_specs=[smem_spec, vmem_spec, smem_spec, vmem_spec] + [any_spec] * 4,
            out_specs=(vmem_spec, any_spec, any_spec),
            scratch_shapes=[
                vmem((blocks, *block), bf),
                vmem((blocks, *block), bf),
                vmem((chip_blocks, *block), bf),
                vmem((2, lanes, *block), bf),
                vmem((2, lanes, *block), bf),
                vmem((per_rank, *block), bf),
                vmem((per_rank, *block), bf),
                vmem((per_rank, *block), bf),
                vmem((ranks, KV, ROWS, HEAD), bf),
                vmem((ranks * ROWS, blocks * tokens), f32),
                vmem((ranks, KV, ROWS, HEAD), f32),
                vmem((ranks, ROWS, HEAD), f32),
                vmem((chips, KV, ROWS, HEAD), f32),
                vmem((chips, ROWS, HEAD), f32),
                vmem((chips, KV, ROWS, HEAD), bf),
                vmem((chips, ROWS, HEAD), f32),
                vmem((chips, KV, ROWS, HEAD), bf),
                vmem((chips, ROWS, HEAD), f32),
                pltpu.SMEM((2, lanes), jnp.int32),
                vmem((KV, ROWS, HEAD), f32),
                vmem((KV, ROWS, HEAD), bf),
                vmem(queries.shape, f32),
                dma((5,)),
                dma,
                dma,
                dma((2 * chips - 1,)),
                dma((ranks,)),
                dma((2, lanes, PIECES)),
                dma((2, lanes, PIECES)),
                dma((2,)),
                dma((2,)),
                dma((2, chips)),
                dma((2, chips)),
                dma,
                dma,
                dma((2,)),
            ],
            compiler_params=pltpu.CompilerParams(
                collective_id=1 + number, has_side_effects=True, vmem_limit_bytes=VMEM_BYTES
            ),
            name="exchange",
        )(*operands)

    pick = pl.pallas_call(
        functools.partial(load_kernel, chips, chip_blocks, rank_slots, choices),
        out_shape=jax.ShapeDtypeStruct((1,), jnp.int32),
        in_specs=[smem_spec],
        out_specs=smem_spec,
        scratch_shapes=[
            vmem((lax.axis_size("grp"), 8, HEAD), jnp.int32),
            dma((lax.axis_size("grp"),)),
            dma((lax.axis_size("grp"),)),
        ],
        compiler_params=pltpu.CompilerParams(collective_id=0, has_side_effects=True),
        name="load",
    )(spill_slots)
    att, newk, newv = lax.switch(
        pick[0],
        [functools.partial(exchange, number, lanes) for number, lanes in enumerate(choices)],
        context_lengths, block_table, spill_slots, queries, prefill_keys, prefill_values, cache_keys, pool_values_prior,
    )

    pool_keys, pool_values, att = pl.pallas_call(
        place_kernel,
        out_shape=(
            jax.ShapeDtypeStruct(cache_keys.shape, bf),
            jax.ShapeDtypeStruct(cache_keys.shape, bf),
            jax.ShapeDtypeStruct(att.shape, bf),
        ),
        in_specs=[smem_spec, smem_spec] + [any_spec] * 4 + [vmem_spec],
        out_specs=(any_spec, any_spec, vmem_spec),
        scratch_shapes=[vmem((2, rank_slots, *block), bf), dma((2, rank_slots)), dma((2, rank_slots))],
        compiler_params=pltpu.CompilerParams(vmem_limit_bytes=VMEM_BYTES),
        name="place",
    )(spill_slots, first.reshape(1), cache_keys, pool_values_prior, newk, newv, att)
    return att, pool_keys, pool_values


def solution(mesh):
    both = ("grp", "blk")
    return jax.shard_map(
        per_device,
        mesh=mesh,
        in_specs=(P(both, None),) + (P(both, None, None),) * 4 + (P("grp"), P("grp", None), P("grp")),
        out_specs=(P(both, None), P(both, None, None), P(both, None, None)),
        check_vma=False,
    )
```

```python
import functools

import jax
import jax.numpy as jnp
from jax import lax
from jax.experimental import pallas as pl
from jax.experimental.pallas import tpu as pltpu
from jax.sharding import PartitionSpec as P

QUERY_HEADS = 40
KV = 8
GROUPS = QUERY_HEADS // KV
HEAD = 128
STEPS = 4
REQ = 4
ROWS = 16
PIECES = 8
HEADS_PER_STEP = 2
LOW = -1e30
FAR = 1 << 24
VMEM_BYTES = 60 * 1024 * 1024
MESH = pl.DeviceIdType.MESH


def lane_plan(spill, chips, z, lanes, chip_blocks, rank_slots):
    total = chips * chip_blocks
    rank_of = [spill[b] // rank_slots for b in range(total)]
    chip_of = [r // 2 for r in rank_of]
    sends, arrivals = [], []
    for way in range(2):
        dest = chip_of if way == 0 else [chips - 1 - c for c in chip_of]
        place = z if way == 0 else chips - 1 - z
        lane_dest = [jnp.int32(-1)] * lanes
        lane_block = [jnp.int32(-1)] * lanes
        send = [jnp.int32(chip_blocks)] * lanes
        arrive = [jnp.int32(-1)] * lanes
        for n in range(chips):
            here = place == n
            if n > 0:
                arrive = [jnp.where(here, lane_block[l], arrive[l]) for l in range(lanes)]
            if n == chips - 1:
                break
            first = (n if way == 0 else chips - 1 - n) * chip_blocks
            left = [dest[first + i] > n for i in range(chip_blocks)]
            for l in reversed(range(min(lanes, chip_blocks * (n + 1)))):
                pick, pick_dest = jnp.int32(chip_blocks), jnp.int32(-1)
                for i in reversed(range(chip_blocks)):
                    pick = jnp.where(left[i], i, pick)
                    pick_dest = jnp.where(left[i], dest[first + i], pick_dest)
                take = (lane_dest[l] <= n) & (pick < chip_blocks)
                left = [left[i] & jnp.logical_not(take & (pick == i)) for i in range(chip_blocks)]
                lane_dest[l] = jnp.where(take, pick_dest, lane_dest[l])
                lane_block[l] = jnp.where(take, first + pick, lane_block[l])
                send[l] = jnp.where(here & take, pick, send[l])
        sends.append(send)
        arrivals.append(arrive)
    return rank_of, sends, arrivals


def blocks_for(rank, rank_of, per_rank):
    found = [jnp.int32(0)] * per_rank
    count = jnp.int32(0)
    for b, target in enumerate(rank_of):
        hit = target == rank
        found = [jnp.where(hit & (count == q), b, found[q]) for q in range(per_rank)]
        count = count + hit.astype(jnp.int32)
    return found


def exchange_kernel(
    chips, lanes, lengths, table, spill, qg, other, pk, pv, ck, cv,
    att, newk, newv,
    kall, vall, own, arr, snd, fin, pout, bias, part, lse, pin_o, pin_l, mo, ml, ro, rl, sched, att_wide,
    loc, lane_s, lane_r, s1_s, s1_r, s2_s, s2_r, fx_s, fx_r, out_s,
):
    rank_slots, tokens, width = ck.shape
    per_rank = pk.shape[0]
    chip_blocks = 2 * per_rank
    blocks = rank_slots + per_rank
    rows_here = STEPS * REQ // (2 * chips)
    piece = tokens // PIECES
    me = lax.axis_index("blk")
    z = me // 2
    core = lax.rem(me, 2)
    partner = 2 * z + 1 - core

    def remote(src, dst, s, r, rank):
        return pltpu.make_async_remote_copy(
            src_ref=src, dst_ref=dst, send_sem=s, recv_sem=r, device_id={"blk": rank}, device_id_type=MESH
        )

    load_kp = pltpu.make_async_copy(pk, kall.at[pl.ds(rank_slots, per_rank)], loc.at[0])
    load_vp = pltpu.make_async_copy(pv, vall.at[pl.ds(rank_slots, per_rank)], loc.at[1])
    load_kc = pltpu.make_async_copy(ck, kall.at[pl.ds(0, rank_slots)], loc.at[2])
    load_vc = pltpu.make_async_copy(cv, vall.at[pl.ds(0, rank_slots)], loc.at[3])
    own_mine = own.at[pl.ds(core * per_rank, per_rank)]

    @pl.when(core == 0)
    def _():
        pltpu.make_async_copy(pk, own_mine, loc.at[4]).start()

    @pl.when(core == 1)
    def _():
        pltpu.make_async_copy(pv, own_mine, loc.at[4]).start()

    load_other = pltpu.make_async_copy(other, own.at[pl.ds((1 - core) * per_rank, per_rank)], loc.at[5])
    load_other.start()
    load_kp.start()
    load_vp.start()
    load_kc.start()
    load_vc.start()

    barrier = pltpu.get_barrier_semaphore()
    pl.semaphore_signal(barrier, inc=1, device_id={"blk": partner}, device_id_type=MESH)
    for off in range(1, chips):
        peer = 2 * lax.rem(z + off, chips) + core
        pl.semaphore_signal(barrier, inc=1, device_id={"blk": peer}, device_id_type=MESH)
    rank_of, sends, arrivals = lane_plan(spill, chips, z, lanes, chip_blocks, rank_slots)
    for way in range(2):
        for l in range(lanes):
            sched[way, l] = sends[way][l]
    pltpu.make_async_copy(pk, own_mine, loc.at[4]).wait()
    load_other.wait()
    pl.semaphore_wait(barrier, chips)

    low_half = z < chips // 2
    near = jnp.where(low_half, z, chips - 1 - z)
    far = chips - 1 - near
    near_way = jnp.where(low_half, 0, 1)
    far_way = 1 - near_way
    near_next = 2 * jnp.where(low_half, z + 1, z - 1) + core
    far_next = 2 * jnp.where(low_half, jnp.maximum(z - 1, 0), jnp.minimum(z + 1, chips - 1)) + core

    def lane_copy(way, l, p, rank):
        rows = pl.ds(p * piece, piece)
        return remote(
            snd.at[way, l, rows], arr.at[way, l, rows], lane_s.at[way, l, p], lane_r.at[way, l, p], rank
        )

    def compose(way, l, p):
        rows = pl.ds(p * piece, piece)
        pick = sched[way, l]
        snd[way, l, rows] = lax.select(
            pick == chip_blocks, arr[way, l, rows], own[jnp.minimum(pick, chip_blocks - 1), rows]
        )

    def compose_own(way, l, p):
        rows = pl.ds(p * piece, piece)
        snd[way, l, rows] = own[jnp.minimum(sched[way, l], chip_blocks - 1), rows]

    def near_step(i):
        l = lanes - 1 - i
        if isinstance(i, int) and l < 0:
            return
        passing = (l >= 0) & (l < chip_blocks * near)
        starting = (l >= 0) & jnp.logical_not(passing) & (l < chip_blocks * (near + 1))

        @pl.when((l >= 0) & (l + 2 < lanes) & (l + 2 < chip_blocks * (near + 1)))
        def _():
            for p in range(PIECES):
                lane_copy(near_way, l + 2, p, near_next).wait_send()

        @pl.when(passing)
        def _():
            for p in range(PIECES):
                lane_copy(near_way, l, p, near_next).wait_recv()
                compose(near_way, l, p)
                lane_copy(near_way, l, p, near_next).start()

        @pl.when(starting)
        def _():
            for p in range(PIECES):
                compose_own(near_way, l, p)
                lane_copy(near_way, l, p, near_next).start()

    def far_step(i):
        l = lanes - 1 - i
        if isinstance(i, int) and l < 0:
            return

        @pl.when((l >= 0) & (far < chips - 1))
        def _():
            for p in range(PIECES):
                lane_copy(far_way, l, p, far_next).wait_recv()
                compose(far_way, l, p)
                lane_copy(far_way, l, p, far_next).start()

    def attend(h):
        cols = pl.ds(pl.multiple_of(h * HEAD, HEAD), HEAD)
        q = qg[:, h].reshape(2 * chips * ROWS, HEAD)
        k = kall[:, :, cols].reshape(blocks * tokens, HEAD)
        v = vall[:, :, cols].reshape(blocks * tokens, HEAD)
        s = lax.dot_general(q, k, (((1,), (1,)), ((), ())), preferred_element_type=jnp.float32)
        s = s * HEAD ** (-0.5) + bias[...]
        m = jnp.max(s, axis=1, keepdims=True)
        w = jnp.exp(s - m)
        total = jnp.sum(w, axis=1, keepdims=True)
        o = jnp.dot(w.astype(jnp.bfloat16), v, preferred_element_type=jnp.float32) / total
        part[:, h] = o.reshape(2 * chips, ROWS, HEAD)
        lane = lax.broadcasted_iota(jnp.int32, (2 * chips, ROWS, HEAD), 2)
        level = (m + jnp.log(total)).reshape(2 * chips, ROWS, 1)
        lse[...] = jnp.where(lane == h, level, lse[...])

    near_step(0)

    row_count = 2 * chips * ROWS
    row = lax.broadcasted_iota(jnp.int32, (row_count, HEAD), 0)
    slot, inner = row // ROWS, row % ROWS
    rank_row = 2 * (slot % chips) + slot // chips
    row_id = rank_row * rows_here + inner % rows_here
    valid = inner < GROUPS * rows_here
    step, request = row_id // REQ, row_id % REQ
    token = lax.broadcasted_iota(jnp.int32, (row_count, HEAD), 1)
    edge = jnp.where(valid, token + (STEPS - 1) - step, FAR).astype(jnp.float32)
    columns = table.shape[1]
    owned = jnp.broadcast_to(table[0:1, :], (row_count, columns))
    length = jnp.full((row_count, columns), lengths[0], jnp.int32)
    for r in range(1, REQ):
        here = request[:, :columns] == r
        owned = jnp.where(here, table[r : r + 1, :], owned)
        length = jnp.where(here, lengths[r], length)
    after = (length - lax.broadcasted_iota(jnp.int32, (row_count, columns), 1) * tokens).astype(jnp.float32)
    for s in range(blocks):
        if s < rank_slots:
            block_id = me * rank_slots + s
            for b in range(chips * chip_blocks):
                block_id = jnp.where(spill[b] == me * rank_slots + s, -1, block_id)
        else:
            block_id = spill[me * per_rank + s - rank_slots]
        bound = jnp.max(jnp.where(owned == block_id, after, float(-FAR)), axis=1, keepdims=True)
        bias[:, pl.ds(s * tokens, tokens)] = jnp.where(edge < bound, 0.0, LOW).astype(jnp.float32)
    lse[...] = jnp.zeros_like(lse)

    load_kp.wait()
    load_vp.wait()
    load_kc.wait()
    load_vc.wait()

    attending = KV // HEADS_PER_STEP

    def mixed(i, carry):
        near_step(i)
        far_step(i - 1)
        for e in range(HEADS_PER_STEP):
            attend((i - 1) * HEADS_PER_STEP + e)
        return carry

    lax.fori_loop(1, 1 + attending, mixed, 0)

    theirs = pl.ds((1 - core) * chips, chips)
    s1_o = remote(part.at[theirs], pin_o, s1_s.at[0], s1_r.at[0], partner)
    s1_l = remote(lse.at[theirs], pin_l, s1_s.at[1], s1_r.at[1], partner)
    s1_o.start()
    s1_l.start()
    near_step(1 + attending)
    far_step(attending)
    s1_o.wait_recv()
    s1_l.wait_recv()

    ours = pl.ds(core * chips, chips)
    level_a, level_b = lse[ours], pin_l[...]
    top = jnp.maximum(level_a, level_b)
    ea, eb = jnp.exp(level_a - top), jnp.exp(level_b - top)
    both = ea + eb
    ml[...] = top + jnp.log(both)
    wa, wb = ea / both, eb / both
    for h in range(KV):
        mixed_rows = part[ours, h] * wa[:, :, h : h + 1] + pin_o[:, h] * wb[:, :, h : h + 1]
        mo[:, h] = mixed_rows.astype(jnp.bfloat16)
    s2 = []
    for off in range(1, chips):
        to = lax.rem(z + off, chips)
        s2.append(remote(mo.at[to], ro.at[z], s2_s.at[0, off], s2_r.at[0, z], 2 * to + core))
        s2.append(remote(ml.at[to], rl.at[z], s2_s.at[1, off], s2_r.at[1, z], 2 * to + core))
    for copy in s2:
        copy.start()
    ro[z] = mo[z]
    rl[z] = ml[z]

    def moving(i, carry):
        near_step(i)
        far_step(i - 1)
        return carry

    if lanes > 2 + attending:
        lax.fori_loop(2 + attending, lanes, moving, 0)
    if lanes > 1 + attending:
        far_step(lanes - 1)

    @pl.when(far == chips - 1)
    def _():
        def drain(i, carry):
            for p in range(PIECES):
                lane_copy(far_way, lanes - 1 - i, p, far_next).wait_recv()
            return carry

        lax.fori_loop(0, lanes, drain, 0)

    def gathered(b, q, target):
        at_home = b // chip_blocks == z
        index = jnp.clip(b - z * chip_blocks, 0, chip_blocks - 1)
        way_of, lane_of = jnp.int32(0), jnp.int32(0)
        for way in range(2):
            for l in range(lanes):
                hit = arrivals[way][l] == b
                way_of = jnp.where(hit, way, way_of)
                lane_of = jnp.where(hit, l, lane_of)
        target[q] = lax.select(at_home, own[index], arr[way_of, lane_of])

    for q, b in enumerate(blocks_for(partner, rank_of, per_rank)):
        gathered(b, q, pout)
    handed = remote(pout, newk, fx_s, fx_r, partner)

    @pl.when(core == 0)
    def _():
        handed.start()

    @pl.when(core == 1)
    def _():
        remote(pout, newv, fx_s, fx_r, partner).start()

    for q, b in enumerate(blocks_for(me, rank_of, per_rank)):
        gathered(b, q, fin)

    @pl.when(core == 0)
    def _():
        pltpu.make_async_copy(fin, newk, out_s).start()

    @pl.when(core == 1)
    def _():
        pltpu.make_async_copy(fin, newv, out_s).start()

    for off in range(1, chips):
        source = lax.rem(z + off, chips)
        remote(mo.at[source], ro.at[source], s2_s.at[0, off], s2_r.at[0, source], partner).wait_recv()
        remote(ml.at[source], rl.at[source], s2_s.at[1, off], s2_r.at[1, source], partner).wait_recv()
    levels = rl[...]
    top = jnp.max(levels, axis=0, keepdims=True)
    shares = jnp.exp(levels - top)
    shares = shares / jnp.sum(shares, axis=0, keepdims=True)
    for h in range(KV):
        rows = jnp.sum(ro[:, h].astype(jnp.float32) * shares[:, :, h : h + 1], axis=0)
        for j in range(GROUPS * rows_here):
            head = h * GROUPS + j // rows_here
            i = j % rows_here
            att_wide[i : i + 1, head * HEAD : (head + 1) * HEAD] = rows[j : j + 1, :]
    att[...] = att_wide[...].astype(jnp.bfloat16)

    handed.wait_recv()

    handed.wait_send()
    s1_o.wait_send()
    s1_l.wait_send()
    for copy in s2:
        copy.wait_send()
    for l in range(2):
        @pl.when(l < chip_blocks * (near + 1))
        def _():
            for p in range(PIECES):
                lane_copy(near_way, l, p, near_next).wait_send()

    @pl.when(far < chips - 1)
    def _():
        def sent(i, carry):
            for p in range(PIECES):
                lane_copy(far_way, i, p, far_next).wait_send()
            return carry

        lax.fori_loop(0, lanes, sent, 0)

    pltpu.make_async_copy(fin, newk, out_s).wait()


def load_kernel(
    chips, chip_blocks, rank_slots, steps, spill, q_in, pk, pv, pick, qg, other,
    box, q_wide, q_ref, send, recv, q_s, q_r, ex_s, ex_r,
):
    groups = lax.axis_size("grp")
    mine = lax.axis_index("grp")
    me = lax.axis_index("blk")
    z = me // 2
    core = lax.rem(me, 2)
    partner = 2 * z + 1 - core
    rows_here = q_in.shape[0]
    barrier = pltpu.get_barrier_semaphore()
    pl.semaphore_signal(barrier, inc=1, device_id={"blk": partner}, device_id_type=MESH)
    for off in range(1, groups):
        pl.semaphore_signal(barrier, inc=1, device_id={"grp": lax.rem(mine + off, groups)}, device_id_type=MESH)
    for off in range(1, chips):
        peer = 2 * lax.rem(z + off, chips) + core
        pl.semaphore_signal(barrier, inc=1, device_id={"blk": peer}, device_id_type=MESH)

    chip_of = [spill[b] // (2 * rank_slots) for b in range(chips * chip_blocks)]
    load = jnp.int32(0)
    for n in range(chips - 1):
        crossing = jnp.int32(0)
        for b in range((n + 1) * chip_blocks):
            crossing = crossing + (chip_of[b] > n).astype(jnp.int32)
        load = jnp.maximum(load, crossing)
    box[mine] = jnp.full(box.shape[1:], load, jnp.int32)
    q_wide[...] = jnp.zeros_like(q_wide)
    q_rows = q_in[...].astype(jnp.float32)
    for h in range(KV):
        for j in range(GROUPS * rows_here):
            head = h * GROUPS + j // rows_here
            i = j % rows_here
            q_wide[h, j : j + 1, :] = q_rows[i : i + 1, head * HEAD : (head + 1) * HEAD]
    q_ref[...] = q_wide[...].astype(jnp.bfloat16)
    pl.semaphore_wait(barrier, groups + chips - 1)

    def copy_to(off, source):
        return pltpu.make_async_remote_copy(
            src_ref=box.at[mine], dst_ref=box.at[mine], send_sem=send.at[off], recv_sem=recv.at[source],
            device_id={"grp": lax.rem(mine + off, groups)}, device_id_type=MESH,
        )

    def remote(src, dst, s, r, rank):
        return pltpu.make_async_remote_copy(
            src_ref=src, dst_ref=dst, send_sem=s, recv_sem=r, device_id={"blk": rank}, device_id_type=MESH
        )

    for off in range(1, groups):
        copy_to(off, mine).start()
    slot = core * chips + z
    q_copies = []
    for off in range(1, chips):
        peer = 2 * lax.rem(z + off, chips) + core
        q_copies.append(remote(q_ref, qg.at[slot], q_s.at[off], q_r.at[slot], peer))
    q_copies.append(remote(q_ref, qg.at[slot], q_s.at[0], q_r.at[slot], partner))
    for copy in q_copies:
        copy.start()

    @pl.when(core == 0)
    def _():
        remote(pv, other, ex_s, ex_r, partner).start()

    @pl.when(core == 1)
    def _():
        remote(pk, other, ex_s, ex_r, partner).start()

    qg[slot] = q_ref[...]
    for off in range(1, groups):
        copy_to(off, lax.rem(mine + off, groups)).wait_recv()
    largest = jnp.max(box[...])
    choice = jnp.int32(0)
    for step in steps[:-1]:
        choice = choice + (largest > step).astype(jnp.int32)
    pick[0] = choice
    for off in range(1, chips):
        came = core * chips + lax.rem(z + off, chips)
        remote(q_ref, qg.at[came], q_s.at[0], q_r.at[came], partner).wait_recv()
        q_copies.append(remote(qg.at[came], qg.at[came], q_s.at[chips - 1 + off], q_r.at[came], partner))
        q_copies[-1].start()
    exchanged = remote(pk, other, ex_s, ex_r, partner)
    exchanged.wait_recv()
    for zz in range(chips):
        came = (1 - core) * chips + zz
        remote(q_ref, qg.at[came], q_s.at[0], q_r.at[came], partner).wait_recv()
    exchanged.wait_send()
    for copy in q_copies:
        copy.wait_send()
    for off in range(1, groups):
        copy_to(off, mine).wait_send()


def place_kernel(spill, first_ref, ck, cv, newk, newv, att_in, pool_k, pool_v, att_out, hold, into, out):
    rank_slots = ck.shape[0]
    first = first_ref[0]
    filled = [jnp.bool_(False)] * rank_slots
    count = jnp.int32(0)
    for b in range(spill.shape[0]):
        at = spill[b] - first
        mine = (at >= 0) & (at < rank_slots)
        filled = [filled[j] | (at == j) for j in range(rank_slots)]
        here, which = jnp.clip(at, 0, rank_slots - 1), jnp.minimum(count, newk.shape[0] - 1)

        @pl.when(mine)
        def _():
            pltpu.make_async_copy(newk.at[which], hold.at[0, here], into.at[0, here]).start()
            pltpu.make_async_copy(newv.at[which], hold.at[1, here], into.at[1, here]).start()

        count = count + mine.astype(jnp.int32)
    for j in range(rank_slots):
        @pl.when(jnp.logical_not(filled[j]))
        def _():
            pltpu.make_async_copy(ck.at[j], hold.at[0, j], into.at[0, j]).start()
            pltpu.make_async_copy(cv.at[j], hold.at[1, j], into.at[1, j]).start()

    att_out[...] = att_in[...]
    stores = []
    for j in range(rank_slots):
        for t, (source, target) in enumerate(((ck, pool_k), (cv, pool_v))):
            pltpu.make_async_copy(source.at[j], hold.at[t, j], into.at[t, j]).wait()
            stores.append(pltpu.make_async_copy(hold.at[t, j], target.at[j], out.at[t, j]))
            stores[-1].start()
    for copy in stores:
        copy.wait()


def per_device(
    queries, cache_keys, pool_values_prior, prefill_keys, prefill_values, context_lengths, block_table, spill_slots
):
    ranks = lax.axis_size("blk")
    chips = ranks // 2
    me = lax.axis_index("blk")
    rank_slots, tokens, width = cache_keys.shape
    per_rank = prefill_keys.shape[0]
    chip_blocks = 2 * per_rank
    blocks = rank_slots + per_rank
    most = chip_blocks * (chips // 2)
    choices = (most // 2, most * 5 // 8, most * 3 // 4, most)
    rows_here, query_width = queries.shape
    first = me * rank_slots

    bf, f32 = jnp.bfloat16, jnp.float32
    vmem = pltpu.VMEM
    dma = pltpu.SemaphoreType.DMA
    any_spec = pl.BlockSpec(memory_space=pl.ANY)
    smem_spec = pl.BlockSpec(memory_space=pltpu.SMEM)
    vmem_spec = pl.BlockSpec(memory_space=pltpu.VMEM)
    block = (tokens, width)
    def exchange(number, lanes, *operands):
        return pl.pallas_call(
            functools.partial(exchange_kernel, chips, lanes),
            out_shape=(
                jax.ShapeDtypeStruct(queries.shape, bf),
                jax.ShapeDtypeStruct((per_rank, *block), bf),
                jax.ShapeDtypeStruct((per_rank, *block), bf),
            ),
            in_specs=[smem_spec, vmem_spec, smem_spec, vmem_spec] + [any_spec] * 5,
            out_specs=(vmem_spec, any_spec, any_spec),
            scratch_shapes=[
                vmem((blocks, *block), bf),
                vmem((blocks, *block), bf),
                vmem((chip_blocks, *block), bf),
                vmem((2, lanes, *block), bf),
                vmem((2, lanes, *block), bf),
                vmem((per_rank, *block), bf),
                vmem((per_rank, *block), bf),
                vmem((ranks * ROWS, blocks * tokens), f32),
                vmem((ranks, KV, ROWS, HEAD), f32),
                vmem((ranks, ROWS, HEAD), f32),
                vmem((chips, KV, ROWS, HEAD), f32),
                vmem((chips, ROWS, HEAD), f32),
                vmem((chips, KV, ROWS, HEAD), bf),
                vmem((chips, ROWS, HEAD), f32),
                vmem((chips, KV, ROWS, HEAD), bf),
                vmem((chips, ROWS, HEAD), f32),
                pltpu.SMEM((2, lanes), jnp.int32),
                vmem(queries.shape, f32),
                dma((6,)),
                dma((2, lanes, PIECES)),
                dma((2, lanes, PIECES)),
                dma((2,)),
                dma((2,)),
                dma((2, chips)),
                dma((2, chips)),
                dma,
                dma,
                dma,
            ],
            compiler_params=pltpu.CompilerParams(
                collective_id=1 + number, has_side_effects=True, vmem_limit_bytes=VMEM_BYTES
            ),
            name="exchange",
        )(*operands)

    pick, gathered_queries, other = pl.pallas_call(
        functools.partial(load_kernel, chips, chip_blocks, rank_slots, choices),
        out_shape=(
            jax.ShapeDtypeStruct((1,), jnp.int32),
            jax.ShapeDtypeStruct((ranks, KV, ROWS, HEAD), bf),
            jax.ShapeDtypeStruct((per_rank, *block), bf),
        ),
        in_specs=[smem_spec, vmem_spec, any_spec, any_spec],
        out_specs=(smem_spec, vmem_spec, vmem_spec),
        scratch_shapes=[
            vmem((lax.axis_size("grp"), 8, HEAD), jnp.int32),
            vmem((KV, ROWS, HEAD), f32),
            vmem((KV, ROWS, HEAD), bf),
            dma((lax.axis_size("grp"),)),
            dma((lax.axis_size("grp"),)),
            dma((2 * chips - 1,)),
            dma((ranks,)),
            dma,
            dma,
        ],
        compiler_params=pltpu.CompilerParams(
            collective_id=0, has_side_effects=True, vmem_limit_bytes=VMEM_BYTES
        ),
        name="load",
    )(spill_slots, queries, prefill_keys, prefill_values)
    att, newk, newv = lax.switch(
        pick[0],
        [functools.partial(exchange, number, lanes) for number, lanes in enumerate(choices)],
        context_lengths, block_table, spill_slots, gathered_queries, other,
        prefill_keys, prefill_values, cache_keys, pool_values_prior,
    )

    pool_keys, pool_values, att = pl.pallas_call(
        place_kernel,
        out_shape=(
            jax.ShapeDtypeStruct(cache_keys.shape, bf),
            jax.ShapeDtypeStruct(cache_keys.shape, bf),
            jax.ShapeDtypeStruct(att.shape, bf),
        ),
        in_specs=[smem_spec, smem_spec] + [any_spec] * 4 + [vmem_spec],
        out_specs=(any_spec, any_spec, vmem_spec),
        scratch_shapes=[vmem((2, rank_slots, *block), bf), dma((2, rank_slots)), dma((2, rank_slots))],
        compiler_params=pltpu.CompilerParams(vmem_limit_bytes=VMEM_BYTES),
        name="place",
    )(spill_slots, first.reshape(1), cache_keys, pool_values_prior, newk, newv, att)
    return att, pool_keys, pool_values


def solution(mesh):
    both = ("grp", "blk")
    return jax.shard_map(
        per_device,
        mesh=mesh,
        in_specs=(P(both, None),) + (P(both, None, None),) * 4 + (P("grp"), P("grp", None), P("grp")),
        out_specs=(P(both, None), P(both, None, None), P(both, None, None)),
        check_vma=False,
    )
```

```python
import functools

import jax
import jax.numpy as jnp
from jax import lax
from jax.experimental import pallas as pl
from jax.experimental.pallas import tpu as pltpu
from jax.sharding import PartitionSpec as P

QUERY_HEADS = 40
KV = 8
GROUPS = QUERY_HEADS // KV
HEAD = 128
STEPS = 4
REQ = 4
ROWS = 16
PIECES = 8
HEADS_PER_STEP = 4
LOW = -1e30
FAR = 1 << 24
VMEM_BYTES = 60 * 1024 * 1024
MESH = pl.DeviceIdType.MESH


def lane_plan(spill, chips, z, lanes, chip_blocks, rank_slots):
    total = chips * chip_blocks
    rank_of = [spill[b] // rank_slots for b in range(total)]
    chip_of = [r // 2 for r in rank_of]
    sends, arrivals = [], []
    for way in range(2):
        dest = chip_of if way == 0 else [chips - 1 - c for c in chip_of]
        place = z if way == 0 else chips - 1 - z
        lane_dest = [jnp.int32(-1)] * lanes
        lane_block = [jnp.int32(-1)] * lanes
        send = [jnp.int32(chip_blocks)] * lanes
        arrive = [jnp.int32(-1)] * lanes
        for n in range(chips):
            here = place == n
            if n > 0:
                arrive = [jnp.where(here, lane_block[l], arrive[l]) for l in range(lanes)]
            if n == chips - 1:
                break
            first = (n if way == 0 else chips - 1 - n) * chip_blocks
            left = [dest[first + i] > n for i in range(chip_blocks)]
            for l in reversed(range(min(lanes, chip_blocks * (n + 1)))):
                pick, pick_dest = jnp.int32(chip_blocks), jnp.int32(-1)
                for i in reversed(range(chip_blocks)):
                    pick = jnp.where(left[i], i, pick)
                    pick_dest = jnp.where(left[i], dest[first + i], pick_dest)
                take = (lane_dest[l] <= n) & (pick < chip_blocks)
                left = [left[i] & jnp.logical_not(take & (pick == i)) for i in range(chip_blocks)]
                lane_dest[l] = jnp.where(take, pick_dest, lane_dest[l])
                lane_block[l] = jnp.where(take, first + pick, lane_block[l])
                send[l] = jnp.where(here & take, pick, send[l])
        sends.append(send)
        arrivals.append(arrive)
    return rank_of, sends, arrivals


def blocks_for(rank, rank_of, per_rank):
    found = [jnp.int32(0)] * per_rank
    count = jnp.int32(0)
    for b, target in enumerate(rank_of):
        hit = target == rank
        found = [jnp.where(hit & (count == q), b, found[q]) for q in range(per_rank)]
        count = count + hit.astype(jnp.int32)
    return found


def exchange_kernel(
    chips, lanes, lengths, table, spill, q_half, other, pk, pv, ck, cv,
    att, newk, newv,
    kall, vall, own, arr, snd, fin, pout, qg, bias, part, lse, pin_o, pin_l, mo, ml, ro, rl, sched, att_wide,
    loc, q_s, q_r, lane_s, lane_r, s1_s, s1_r, s2_s, s2_r, fx_s, fx_r, out_s,
):
    rank_slots, tokens, width = ck.shape
    per_rank = pk.shape[0]
    chip_blocks = 2 * per_rank
    blocks = rank_slots + per_rank
    rows_here = STEPS * REQ // (2 * chips)
    piece = tokens // PIECES
    me = lax.axis_index("blk")
    z = me // 2
    core = lax.rem(me, 2)
    partner = 2 * z + 1 - core

    def remote(src, dst, s, r, rank):
        return pltpu.make_async_remote_copy(
            src_ref=src, dst_ref=dst, send_sem=s, recv_sem=r, device_id={"blk": rank}, device_id_type=MESH
        )

    load_kp = pltpu.make_async_copy(pk, kall.at[pl.ds(rank_slots, per_rank)], loc.at[0])
    load_vp = pltpu.make_async_copy(pv, vall.at[pl.ds(rank_slots, per_rank)], loc.at[1])
    load_kc = pltpu.make_async_copy(ck, kall.at[pl.ds(0, rank_slots)], loc.at[2])
    load_vc = pltpu.make_async_copy(cv, vall.at[pl.ds(0, rank_slots)], loc.at[3])
    own_mine = own.at[pl.ds(core * per_rank, per_rank)]

    @pl.when(core == 0)
    def _():
        pltpu.make_async_copy(pk, own_mine, loc.at[4]).start()

    @pl.when(core == 1)
    def _():
        pltpu.make_async_copy(pv, own_mine, loc.at[4]).start()

    load_other = pltpu.make_async_copy(other, own.at[pl.ds((1 - core) * per_rank, per_rank)], loc.at[5])
    load_other.start()
    load_kp.start()
    load_vp.start()
    load_kc.start()
    load_vc.start()

    barrier = pltpu.get_barrier_semaphore()
    pl.semaphore_signal(barrier, inc=1, device_id={"blk": partner}, device_id_type=MESH)
    for off in range(1, chips):
        peer = 2 * lax.rem(z + off, chips) + core
        pl.semaphore_signal(barrier, inc=1, device_id={"blk": peer}, device_id_type=MESH)
    rank_of, sends, arrivals = lane_plan(spill, chips, z, lanes, chip_blocks, rank_slots)
    for way in range(2):
        for l in range(lanes):
            sched[way, l] = sends[way][l]
    pltpu.make_async_copy(pk, own_mine, loc.at[4]).wait()
    load_other.wait()
    pl.semaphore_wait(barrier, chips)
    ours = pl.ds(core * chips, chips)
    q_copy = remote(q_half, qg.at[ours], q_s, q_r, partner)
    q_copy.start()

    low_half = z < chips // 2
    near = jnp.where(low_half, z, chips - 1 - z)
    far = chips - 1 - near
    near_way = jnp.where(low_half, 0, 1)
    far_way = 1 - near_way
    near_next = 2 * jnp.where(low_half, z + 1, z - 1) + core
    far_next = 2 * jnp.where(low_half, jnp.maximum(z - 1, 0), jnp.minimum(z + 1, chips - 1)) + core

    def lane_copy(way, l, p, rank):
        rows = pl.ds(p * piece, piece)
        return remote(
            snd.at[way, l, rows], arr.at[way, l, rows], lane_s.at[way, l, p], lane_r.at[way, l, p], rank
        )

    def compose(way, l, p):
        rows = pl.ds(p * piece, piece)
        pick = sched[way, l]
        snd[way, l, rows] = lax.select(
            pick == chip_blocks, arr[way, l, rows], own[jnp.minimum(pick, chip_blocks - 1), rows]
        )

    def compose_own(way, l, p):
        rows = pl.ds(p * piece, piece)
        snd[way, l, rows] = own[jnp.minimum(sched[way, l], chip_blocks - 1), rows]

    def near_step(i):
        l = lanes - 1 - i
        if isinstance(i, int) and l < 0:
            return
        passing = (l >= 0) & (l < chip_blocks * near)
        starting = (l >= 0) & jnp.logical_not(passing) & (l < chip_blocks * (near + 1))

        @pl.when((l >= 0) & (l + 2 < lanes) & (l + 2 < chip_blocks * (near + 1)))
        def _():
            for p in range(PIECES):
                lane_copy(near_way, l + 2, p, near_next).wait_send()

        @pl.when(passing)
        def _():
            for p in range(PIECES):
                lane_copy(near_way, l, p, near_next).wait_recv()
                compose(near_way, l, p)
                lane_copy(near_way, l, p, near_next).start()

        @pl.when(starting)
        def _():
            for p in range(PIECES):
                compose_own(near_way, l, p)
                lane_copy(near_way, l, p, near_next).start()

    def far_step(i):
        l = lanes - 1 - i
        if isinstance(i, int) and l < 0:
            return

        @pl.when((l >= 0) & (far < chips - 1))
        def _():
            for p in range(PIECES):
                lane_copy(far_way, l, p, far_next).wait_recv()
                compose(far_way, l, p)
                lane_copy(far_way, l, p, far_next).start()

    def attend(h, carry):
        cols = pl.ds(pl.multiple_of(h * HEAD, HEAD), HEAD)
        q = qg[:, h].reshape(2 * chips * ROWS, HEAD)
        k = kall[:, :, cols].reshape(blocks * tokens, HEAD)
        v = vall[:, :, cols].reshape(blocks * tokens, HEAD)
        s = lax.dot_general(q, k, (((1,), (1,)), ((), ())), preferred_element_type=jnp.float32)
        s = s * HEAD ** (-0.5) + bias[...]
        m = jnp.max(s, axis=1, keepdims=True)
        w = jnp.exp(s - m)
        total = jnp.sum(w, axis=1, keepdims=True)
        o = jnp.dot(w.astype(jnp.bfloat16), v, preferred_element_type=jnp.float32) / total
        part[:, h] = o.reshape(2 * chips, ROWS, HEAD)
        lane = lax.broadcasted_iota(jnp.int32, (2 * chips, ROWS, HEAD), 2)
        level = (m + jnp.log(total)).reshape(2 * chips, ROWS, 1)
        lse[...] = jnp.where(lane == h, level, lse[...])
        return carry

    near_step(0)
    qg[ours] = q_half[...]

    row_count = 2 * chips * ROWS
    row = lax.broadcasted_iota(jnp.int32, (row_count, HEAD), 0)
    slot, inner = row // ROWS, row % ROWS
    rank_row = 2 * (slot % chips) + slot // chips
    row_id = rank_row * rows_here + inner % rows_here
    valid = inner < GROUPS * rows_here
    step, request = row_id // REQ, row_id % REQ
    token = lax.broadcasted_iota(jnp.int32, (row_count, HEAD), 1)
    edge = jnp.where(valid, token + (STEPS - 1) - step, FAR).astype(jnp.float32)
    columns = table.shape[1]
    owned = jnp.broadcast_to(table[0:1, :], (row_count, columns))
    length = jnp.full((row_count, columns), lengths[0], jnp.int32)
    for r in range(1, REQ):
        here = request[:, :columns] == r
        owned = jnp.where(here, table[r : r + 1, :], owned)
        length = jnp.where(here, lengths[r], length)
    after = (length - lax.broadcasted_iota(jnp.int32, (row_count, columns), 1) * tokens).astype(jnp.float32)
    for s in range(blocks):
        if s < rank_slots:
            block_id = me * rank_slots + s
            for b in range(chips * chip_blocks):
                block_id = jnp.where(spill[b] == me * rank_slots + s, -1, block_id)
        else:
            block_id = spill[me * per_rank + s - rank_slots]
        bound = jnp.max(jnp.where(owned == block_id, after, float(-FAR)), axis=1, keepdims=True)
        bias[:, pl.ds(s * tokens, tokens)] = jnp.where(edge < bound, 0.0, LOW).astype(jnp.float32)
    lse[...] = jnp.zeros_like(lse)

    load_kp.wait()
    load_vp.wait()
    load_kc.wait()
    load_vc.wait()
    q_copy.wait()

    attending = KV // HEADS_PER_STEP

    def mixed(i, carry):
        near_step(i)
        lax.fori_loop((i - 1) * HEADS_PER_STEP, i * HEADS_PER_STEP, attend, 0)
        far_step(i - 1)
        return carry

    lax.fori_loop(1, 1 + attending, mixed, 0)

    theirs = pl.ds((1 - core) * chips, chips)
    s1_o = remote(part.at[theirs], pin_o, s1_s.at[0], s1_r.at[0], partner)
    s1_l = remote(lse.at[theirs], pin_l, s1_s.at[1], s1_r.at[1], partner)
    s1_o.start()
    s1_l.start()
    near_step(1 + attending)
    s1_o.wait_recv()
    s1_l.wait_recv()

    level_a, level_b = lse[ours], pin_l[...]
    top = jnp.maximum(level_a, level_b)
    ea, eb = jnp.exp(level_a - top), jnp.exp(level_b - top)
    both = ea + eb
    ml[...] = top + jnp.log(both)
    wa, wb = ea / both, eb / both
    for h in range(KV):
        mixed_rows = part[ours, h] * wa[:, :, h : h + 1] + pin_o[:, h] * wb[:, :, h : h + 1]
        mo[:, h] = mixed_rows.astype(jnp.bfloat16)
    s2 = []
    for off in range(1, chips):
        to = lax.rem(z + off, chips)
        s2.append(remote(mo.at[to], ro.at[z], s2_s.at[0, off], s2_r.at[0, z], 2 * to + core))
        s2.append(remote(ml.at[to], rl.at[z], s2_s.at[1, off], s2_r.at[1, z], 2 * to + core))
    for copy in s2:
        copy.start()
    ro[z] = mo[z]
    rl[z] = ml[z]
    far_step(attending)

    def moving(i, carry):
        near_step(i)
        far_step(i - 1)
        return carry

    if lanes > 2 + attending:
        lax.fori_loop(2 + attending, lanes, moving, 0)
    if lanes > 1 + attending:
        far_step(lanes - 1)

    @pl.when(far == chips - 1)
    def _():
        def drain(i, carry):
            for p in range(PIECES):
                lane_copy(far_way, lanes - 1 - i, p, far_next).wait_recv()
            return carry

        lax.fori_loop(0, lanes, drain, 0)

    def gathered(b, q, target):
        at_home = b // chip_blocks == z
        index = jnp.clip(b - z * chip_blocks, 0, chip_blocks - 1)
        way_of, lane_of = jnp.int32(0), jnp.int32(0)
        for way in range(2):
            for l in range(lanes):
                hit = arrivals[way][l] == b
                way_of = jnp.where(hit, way, way_of)
                lane_of = jnp.where(hit, l, lane_of)
        target[q] = lax.select(at_home, own[index], arr[way_of, lane_of])

    for q, b in enumerate(blocks_for(partner, rank_of, per_rank)):
        gathered(b, q, pout)
    handed = remote(pout, newk, fx_s, fx_r, partner)

    @pl.when(core == 0)
    def _():
        handed.start()

    @pl.when(core == 1)
    def _():
        remote(pout, newv, fx_s, fx_r, partner).start()

    for q, b in enumerate(blocks_for(me, rank_of, per_rank)):
        gathered(b, q, fin)

    @pl.when(core == 0)
    def _():
        pltpu.make_async_copy(fin, newk, out_s).start()

    @pl.when(core == 1)
    def _():
        pltpu.make_async_copy(fin, newv, out_s).start()

    for off in range(1, chips):
        source = lax.rem(z + off, chips)
        remote(mo.at[source], ro.at[source], s2_s.at[0, off], s2_r.at[0, source], partner).wait_recv()
        remote(ml.at[source], rl.at[source], s2_s.at[1, off], s2_r.at[1, source], partner).wait_recv()
    levels = rl[...]
    top = jnp.max(levels, axis=0, keepdims=True)
    shares = jnp.exp(levels - top)
    shares = shares / jnp.sum(shares, axis=0, keepdims=True)
    for h in range(KV):
        rows = jnp.sum(ro[:, h].astype(jnp.float32) * shares[:, :, h : h + 1], axis=0)
        for j in range(GROUPS * rows_here):
            head = h * GROUPS + j // rows_here
            i = j % rows_here
            att_wide[i : i + 1, head * HEAD : (head + 1) * HEAD] = rows[j : j + 1, :]
    att[...] = att_wide[...].astype(jnp.bfloat16)

    handed.wait_recv()

    handed.wait_send()
    s1_o.wait_send()
    s1_l.wait_send()
    for copy in s2:
        copy.wait_send()
    for l in range(2):
        @pl.when(l < chip_blocks * (near + 1))
        def _():
            for p in range(PIECES):
                lane_copy(near_way, l, p, near_next).wait_send()

    @pl.when(far < chips - 1)
    def _():
        def sent(i, carry):
            for p in range(PIECES):
                lane_copy(far_way, i, p, far_next).wait_send()
            return carry

        lax.fori_loop(0, lanes, sent, 0)

    pltpu.make_async_copy(fin, newk, out_s).wait()


def load_kernel(
    chips, chip_blocks, rank_slots, steps, spill, q_in, pk, pv, pick, qg, other,
    box, q_wide, q_ref, send, recv, q_s, q_r, ex_s, ex_r,
):
    groups = lax.axis_size("grp")
    mine = lax.axis_index("grp")
    me = lax.axis_index("blk")
    z = me // 2
    core = lax.rem(me, 2)
    partner = 2 * z + 1 - core
    rows_here = q_in.shape[0]
    barrier = pltpu.get_barrier_semaphore()
    pl.semaphore_signal(barrier, inc=1, device_id={"blk": partner}, device_id_type=MESH)
    for off in range(1, groups):
        pl.semaphore_signal(barrier, inc=1, device_id={"grp": lax.rem(mine + off, groups)}, device_id_type=MESH)
    for off in range(1, chips):
        peer = 2 * lax.rem(z + off, chips) + core
        pl.semaphore_signal(barrier, inc=1, device_id={"blk": peer}, device_id_type=MESH)

    chip_of = [spill[b] // (2 * rank_slots) for b in range(chips * chip_blocks)]
    load = jnp.int32(0)
    for n in range(chips - 1):
        crossing = jnp.int32(0)
        for b in range((n + 1) * chip_blocks):
            crossing = crossing + (chip_of[b] > n).astype(jnp.int32)
        load = jnp.maximum(load, crossing)
    box[mine] = jnp.full(box.shape[1:], load, jnp.int32)
    q_wide[...] = jnp.zeros_like(q_wide)
    q_rows = q_in[...].astype(jnp.float32)
    for h in range(KV):
        for j in range(GROUPS * rows_here):
            head = h * GROUPS + j // rows_here
            i = j % rows_here
            q_wide[h, j : j + 1, :] = q_rows[i : i + 1, head * HEAD : (head + 1) * HEAD]
    q_ref[...] = q_wide[...].astype(jnp.bfloat16)
    pl.semaphore_wait(barrier, groups + chips - 1)

    def copy_to(off, source):
        return pltpu.make_async_remote_copy(
            src_ref=box.at[mine], dst_ref=box.at[mine], send_sem=send.at[off], recv_sem=recv.at[source],
            device_id={"grp": lax.rem(mine + off, groups)}, device_id_type=MESH,
        )

    def remote(src, dst, s, r, rank):
        return pltpu.make_async_remote_copy(
            src_ref=src, dst_ref=dst, send_sem=s, recv_sem=r, device_id={"blk": rank}, device_id_type=MESH
        )

    for off in range(1, groups):
        copy_to(off, mine).start()
    q_copies = []
    for off in range(1, chips):
        peer = 2 * lax.rem(z + off, chips) + core
        q_copies.append(remote(q_ref, qg.at[z], q_s.at[off], q_r.at[z], peer))
    for copy in q_copies:
        copy.start()

    @pl.when(core == 0)
    def _():
        remote(pv, other, ex_s, ex_r, partner).start()

    @pl.when(core == 1)
    def _():
        remote(pk, other, ex_s, ex_r, partner).start()

    qg[z] = q_ref[...]
    for off in range(1, groups):
        copy_to(off, lax.rem(mine + off, groups)).wait_recv()
    largest = jnp.max(box[...])
    choice = jnp.int32(0)
    for step in steps[:-1]:
        choice = choice + (largest > step).astype(jnp.int32)
    pick[0] = choice
    for off in range(1, chips):
        came = lax.rem(z + off, chips)
        remote(q_ref, qg.at[came], q_s.at[off], q_r.at[came], partner).wait_recv()
    exchanged = remote(pk, other, ex_s, ex_r, partner)
    exchanged.wait_recv()
    exchanged.wait_send()
    for copy in q_copies:
        copy.wait_send()
    for off in range(1, groups):
        copy_to(off, mine).wait_send()


def place_kernel(spill, first_ref, ck, cv, newk, newv, att_in, pool_k, pool_v, att_out, hold, into, out):
    rank_slots = ck.shape[0]
    first = first_ref[0]
    filled = [jnp.bool_(False)] * rank_slots
    count = jnp.int32(0)
    for b in range(spill.shape[0]):
        at = spill[b] - first
        mine = (at >= 0) & (at < rank_slots)
        filled = [filled[j] | (at == j) for j in range(rank_slots)]
        here, which = jnp.clip(at, 0, rank_slots - 1), jnp.minimum(count, newk.shape[0] - 1)

        @pl.when(mine)
        def _():
            pltpu.make_async_copy(newk.at[which], hold.at[0, here], into.at[0, here]).start()
            pltpu.make_async_copy(newv.at[which], hold.at[1, here], into.at[1, here]).start()

        count = count + mine.astype(jnp.int32)
    for j in range(rank_slots):
        @pl.when(jnp.logical_not(filled[j]))
        def _():
            pltpu.make_async_copy(ck.at[j], hold.at[0, j], into.at[0, j]).start()
            pltpu.make_async_copy(cv.at[j], hold.at[1, j], into.at[1, j]).start()

    att_out[...] = att_in[...]
    stores = []
    for j in range(rank_slots):
        for t, (source, target) in enumerate(((ck, pool_k), (cv, pool_v))):
            pltpu.make_async_copy(source.at[j], hold.at[t, j], into.at[t, j]).wait()
            stores.append(pltpu.make_async_copy(hold.at[t, j], target.at[j], out.at[t, j]))
            stores[-1].start()
    for copy in stores:
        copy.wait()


def per_device(
    queries, cache_keys, pool_values_prior, prefill_keys, prefill_values, context_lengths, block_table, spill_slots
):
    ranks = lax.axis_size("blk")
    chips = ranks // 2
    me = lax.axis_index("blk")
    rank_slots, tokens, width = cache_keys.shape
    per_rank = prefill_keys.shape[0]
    chip_blocks = 2 * per_rank
    blocks = rank_slots + per_rank
    most = chip_blocks * (chips // 2)
    choices = (most // 2, most * 5 // 8, most * 3 // 4, most)
    rows_here, query_width = queries.shape
    first = me * rank_slots

    bf, f32 = jnp.bfloat16, jnp.float32
    vmem = pltpu.VMEM
    dma = pltpu.SemaphoreType.DMA
    any_spec = pl.BlockSpec(memory_space=pl.ANY)
    smem_spec = pl.BlockSpec(memory_space=pltpu.SMEM)
    vmem_spec = pl.BlockSpec(memory_space=pltpu.VMEM)
    block = (tokens, width)
    def exchange(number, lanes, *operands):
        return pl.pallas_call(
            functools.partial(exchange_kernel, chips, lanes),
            out_shape=(
                jax.ShapeDtypeStruct(queries.shape, bf),
                jax.ShapeDtypeStruct((per_rank, *block), bf),
                jax.ShapeDtypeStruct((per_rank, *block), bf),
            ),
            in_specs=[smem_spec, vmem_spec, smem_spec, vmem_spec] + [any_spec] * 5,
            out_specs=(vmem_spec, any_spec, any_spec),
            scratch_shapes=[
                vmem((blocks, *block), bf),
                vmem((blocks, *block), bf),
                vmem((chip_blocks, *block), bf),
                vmem((2, lanes, *block), bf),
                vmem((2, lanes, *block), bf),
                vmem((per_rank, *block), bf),
                vmem((per_rank, *block), bf),
                vmem((ranks, KV, ROWS, HEAD), bf),
                vmem((ranks * ROWS, blocks * tokens), f32),
                vmem((ranks, KV, ROWS, HEAD), f32),
                vmem((ranks, ROWS, HEAD), f32),
                vmem((chips, KV, ROWS, HEAD), f32),
                vmem((chips, ROWS, HEAD), f32),
                vmem((chips, KV, ROWS, HEAD), bf),
                vmem((chips, ROWS, HEAD), f32),
                vmem((chips, KV, ROWS, HEAD), bf),
                vmem((chips, ROWS, HEAD), f32),
                pltpu.SMEM((2, lanes), jnp.int32),
                vmem(queries.shape, f32),
                dma((6,)),
                dma,
                dma,
                dma((2, lanes, PIECES)),
                dma((2, lanes, PIECES)),
                dma((2,)),
                dma((2,)),
                dma((2, chips)),
                dma((2, chips)),
                dma,
                dma,
                dma,
            ],
            compiler_params=pltpu.CompilerParams(
                collective_id=1 + number, has_side_effects=True, vmem_limit_bytes=VMEM_BYTES
            ),
            name="exchange",
        )(*operands)

    pick, gathered_queries, other = pl.pallas_call(
        functools.partial(load_kernel, chips, chip_blocks, rank_slots, choices),
        out_shape=(
            jax.ShapeDtypeStruct((1,), jnp.int32),
            jax.ShapeDtypeStruct((chips, KV, ROWS, HEAD), bf),
            jax.ShapeDtypeStruct((per_rank, *block), bf),
        ),
        in_specs=[smem_spec, vmem_spec, any_spec, any_spec],
        out_specs=(smem_spec, vmem_spec, vmem_spec),
        scratch_shapes=[
            vmem((lax.axis_size("grp"), 8, HEAD), jnp.int32),
            vmem((KV, ROWS, HEAD), f32),
            vmem((KV, ROWS, HEAD), bf),
            dma((lax.axis_size("grp"),)),
            dma((lax.axis_size("grp"),)),
            dma((chips,)),
            dma((chips,)),
            dma,
            dma,
        ],
        compiler_params=pltpu.CompilerParams(
            collective_id=0, has_side_effects=True, vmem_limit_bytes=VMEM_BYTES
        ),
        name="load",
    )(spill_slots, queries, prefill_keys, prefill_values)
    att, newk, newv = lax.switch(
        pick[0],
        [functools.partial(exchange, number, lanes) for number, lanes in enumerate(choices)],
        context_lengths, block_table, spill_slots, gathered_queries, other,
        prefill_keys, prefill_values, cache_keys, pool_values_prior,
    )

    pool_keys, pool_values, att = pl.pallas_call(
        place_kernel,
        out_shape=(
            jax.ShapeDtypeStruct(cache_keys.shape, bf),
            jax.ShapeDtypeStruct(cache_keys.shape, bf),
            jax.ShapeDtypeStruct(att.shape, bf),
        ),
        in_specs=[smem_spec, smem_spec] + [any_spec] * 4 + [vmem_spec],
        out_specs=(any_spec, any_spec, vmem_spec),
        scratch_shapes=[vmem((2, rank_slots, *block), bf), dma((2, rank_slots)), dma((2, rank_slots))],
        compiler_params=pltpu.CompilerParams(vmem_limit_bytes=VMEM_BYTES),
        name="place",
    )(spill_slots, first.reshape(1), cache_keys, pool_values_prior, newk, newv, att)
    return att, pool_keys, pool_values


def solution(mesh):
    both = ("grp", "blk")
    return jax.shard_map(
        per_device,
        mesh=mesh,
        in_specs=(P(both, None),) + (P(both, None, None),) * 4 + (P("grp"), P("grp", None), P("grp")),
        out_specs=(P(both, None), P(both, None, None), P(both, None, None)),
        check_vma=False,
    )
```

```python
import functools

import jax
import jax.numpy as jnp
from jax import lax
from jax.experimental import pallas as pl
from jax.experimental.pallas import tpu as pltpu
from jax.sharding import PartitionSpec as P

QUERY_HEADS = 40
KV = 8
GROUPS = QUERY_HEADS // KV
HEAD = 128
STEPS = 4
REQ = 4
ROWS = 16
PIECES = 8
HEADS_PER_STEP = 2
LOW = -1e30
FAR = 1 << 24
VMEM_BYTES = 60 * 1024 * 1024
MESH = pl.DeviceIdType.MESH


def lane_plan(spill, chips, z, lanes, chip_blocks, rank_slots):
    total = chips * chip_blocks
    rank_of = [lax.div(spill[b], jnp.int32(rank_slots)) for b in range(total)]
    chip_of = [r >> 1 for r in rank_of]
    sends, arrivals = [], []
    for way in range(2):
        dest = chip_of if way == 0 else [chips - 1 - c for c in chip_of]
        place = z if way == 0 else chips - 1 - z
        lane_dest = [jnp.int32(-1)] * lanes
        lane_block = [jnp.int32(-1)] * lanes
        send = [jnp.int32(chip_blocks)] * lanes
        arrive = [jnp.int32(-1)] * lanes
        for n in range(chips):
            here = place == n
            if n > 0:
                arrive = [jnp.where(here, lane_block[l], arrive[l]) for l in range(lanes)]
            if n == chips - 1:
                break
            first = (n if way == 0 else chips - 1 - n) * chip_blocks
            left = [dest[first + i] > n for i in range(chip_blocks)]
            for l in reversed(range(min(lanes, chip_blocks * (n + 1)))):
                pick, pick_dest = jnp.int32(chip_blocks), jnp.int32(-1)
                for i in reversed(range(chip_blocks)):
                    pick = jnp.where(left[i], i, pick)
                    pick_dest = jnp.where(left[i], dest[first + i], pick_dest)
                take = (lane_dest[l] <= n) & (pick < chip_blocks)
                left = [left[i] & jnp.logical_not(take & (pick == i)) for i in range(chip_blocks)]
                lane_dest[l] = jnp.where(take, pick_dest, lane_dest[l])
                lane_block[l] = jnp.where(take, first + pick, lane_block[l])
                send[l] = jnp.where(here & take, pick, send[l])
        sends.append(send)
        arrivals.append(arrive)
    return rank_of, sends, arrivals


def blocks_for(rank, rank_of, per_rank):
    found = [jnp.int32(0)] * per_rank
    count = jnp.int32(0)
    for b, target in enumerate(rank_of):
        hit = target == rank
        found = [jnp.where(hit & (count == q), b, found[q]) for q in range(per_rank)]
        count = count + hit.astype(jnp.int32)
    return found


def exchange_kernel(
    chips, lanes, lengths, table, spill, q_half, other, pk, pv, ck, cv,
    att, newk, newv,
    kall, vall, own, arr, snd, fin, pout, qg, bias, part, lse, pin_o, pin_l, mo, ml, ro, rl, sched, att_wide,
    loc, q_s, q_r, lane_s, lane_r, s1_s, s1_r, s2_s, s2_r, fx_s, fx_r, out_s,
):
    rank_slots, tokens, width = ck.shape
    per_rank = pk.shape[0]
    chip_blocks = 2 * per_rank
    blocks = rank_slots + per_rank
    rows_here = STEPS * REQ // (2 * chips)
    piece = tokens // PIECES
    me = lax.axis_index("blk")
    z = me // 2
    core = lax.rem(me, 2)
    partner = 2 * z + 1 - core

    def remote(src, dst, s, r, rank):
        return pltpu.make_async_remote_copy(
            src_ref=src, dst_ref=dst, send_sem=s, recv_sem=r, device_id={"blk": rank}, device_id_type=MESH
        )

    load_kp = pltpu.make_async_copy(pk, kall.at[pl.ds(rank_slots, per_rank)], loc.at[0])
    load_vp = pltpu.make_async_copy(pv, vall.at[pl.ds(rank_slots, per_rank)], loc.at[1])
    load_kc = pltpu.make_async_copy(ck, kall.at[pl.ds(0, rank_slots)], loc.at[2])
    load_vc = pltpu.make_async_copy(cv, vall.at[pl.ds(0, rank_slots)], loc.at[3])
    own_mine = own.at[pl.ds(core * per_rank, per_rank)]

    @pl.when(core == 0)
    def _():
        pltpu.make_async_copy(pk, own_mine, loc.at[4]).start()

    @pl.when(core == 1)
    def _():
        pltpu.make_async_copy(pv, own_mine, loc.at[4]).start()

    load_other = pltpu.make_async_copy(other, own.at[pl.ds((1 - core) * per_rank, per_rank)], loc.at[5])
    load_other.start()
    load_kp.start()
    load_vp.start()
    load_kc.start()
    load_vc.start()

    barrier = pltpu.get_barrier_semaphore()
    pl.semaphore_signal(barrier, inc=1, device_id={"blk": partner}, device_id_type=MESH)
    for off in range(1, chips):
        peer = 2 * lax.rem(z + off, chips) + core
        pl.semaphore_signal(barrier, inc=1, device_id={"blk": peer}, device_id_type=MESH)
    rank_of, sends, arrivals = lane_plan(spill, chips, z, lanes, chip_blocks, rank_slots)
    for way in range(2):
        for l in range(lanes):
            sched[way, l] = sends[way][l]
    pltpu.make_async_copy(pk, own_mine, loc.at[4]).wait()
    load_other.wait()
    pl.semaphore_wait(barrier, chips)
    ours = pl.ds(core * chips, chips)
    q_copy = remote(q_half, qg.at[ours], q_s, q_r, partner)
    q_copy.start()

    low_half = z < chips // 2
    near = jnp.where(low_half, z, chips - 1 - z)
    far = chips - 1 - near
    near_way = jnp.where(low_half, 0, 1)
    far_way = 1 - near_way
    near_next = 2 * jnp.where(low_half, z + 1, z - 1) + core
    far_next = 2 * jnp.where(low_half, jnp.maximum(z - 1, 0), jnp.minimum(z + 1, chips - 1)) + core

    def lane_copy(way, l, p, rank):
        rows = pl.ds(p * piece, piece)
        return remote(
            snd.at[way, l, rows], arr.at[way, l, rows], lane_s.at[way, l, p], lane_r.at[way, l, p], rank
        )

    def compose(way, l, p):
        rows = pl.ds(p * piece, piece)
        pick = sched[way, l]
        snd[way, l, rows] = lax.select(
            pick == chip_blocks, arr[way, l, rows], own[jnp.minimum(pick, chip_blocks - 1), rows]
        )

    def compose_own(way, l, p):
        rows = pl.ds(p * piece, piece)
        snd[way, l, rows] = own[jnp.minimum(sched[way, l], chip_blocks - 1), rows]

    def near_step(i):
        l = lanes - 1 - i
        if isinstance(i, int) and l < 0:
            return
        passing = (l >= 0) & (l < chip_blocks * near)
        starting = (l >= 0) & jnp.logical_not(passing) & (l < chip_blocks * (near + 1))

        @pl.when((l >= 0) & (l + 2 < lanes) & (l + 2 < chip_blocks * (near + 1)))
        def _():
            for p in range(PIECES):
                lane_copy(near_way, l + 2, p, near_next).wait_send()

        @pl.when(passing)
        def _():
            for p in range(PIECES):
                lane_copy(near_way, l, p, near_next).wait_recv()
                compose(near_way, l, p)
                lane_copy(near_way, l, p, near_next).start()

        @pl.when(starting)
        def _():
            for p in range(PIECES):
                compose_own(near_way, l, p)
                lane_copy(near_way, l, p, near_next).start()

    def far_step(i):
        l = lanes - 1 - i
        if isinstance(i, int) and l < 0:
            return

        @pl.when((l >= 0) & (far < chips - 1))
        def _():
            for p in range(PIECES):
                lane_copy(far_way, l, p, far_next).wait_recv()
                compose(far_way, l, p)
                lane_copy(far_way, l, p, far_next).start()

    def attend(h):
        cols = pl.ds(pl.multiple_of(h * HEAD, HEAD), HEAD)
        q = qg[:, h].reshape(2 * chips * ROWS, HEAD)
        k = kall[:, :, cols].reshape(blocks * tokens, HEAD)
        v = vall[:, :, cols].reshape(blocks * tokens, HEAD)
        s = lax.dot_general(q, k, (((1,), (1,)), ((), ())), preferred_element_type=jnp.float32)
        s = s * HEAD ** (-0.5) + bias[...]
        m = jnp.max(s, axis=1, keepdims=True)
        w = jnp.exp(s - m)
        total = jnp.sum(w, axis=1, keepdims=True)
        o = jnp.dot(w.astype(jnp.bfloat16), v, preferred_element_type=jnp.float32) / total
        part[:, h] = o.reshape(2 * chips, ROWS, HEAD)
        lane = lax.broadcasted_iota(jnp.int32, (2 * chips, ROWS, HEAD), 2)
        level = (m + jnp.log(total)).reshape(2 * chips, ROWS, 1)
        lse[...] = jnp.where(lane == h, level, lse[...])

    near_step(0)
    qg[ours] = q_half[...]

    row_count = 2 * chips * ROWS
    row = lax.broadcasted_iota(jnp.int32, (row_count, HEAD), 0)
    slot, inner = row >> (ROWS.bit_length() - 1), row & (ROWS - 1)
    rank_row = 2 * (slot & (chips - 1)) + (slot >> (chips.bit_length() - 1))
    row_id = rank_row * rows_here + (inner & (rows_here - 1))
    valid = inner < GROUPS * rows_here
    step, request = row_id >> (REQ.bit_length() - 1), row_id & (REQ - 1)
    token = lax.broadcasted_iota(jnp.int32, (row_count, HEAD), 1)
    edge = jnp.where(valid, token + (STEPS - 1) - step, FAR).astype(jnp.float32)
    columns = table.shape[1]
    owned = jnp.broadcast_to(table[0:1, :], (row_count, columns))
    length = jnp.full((row_count, columns), lengths[0], jnp.int32)
    for r in range(1, REQ):
        here = request[:, :columns] == r
        owned = jnp.where(here, table[r : r + 1, :], owned)
        length = jnp.where(here, lengths[r], length)
    after = (length - lax.broadcasted_iota(jnp.int32, (row_count, columns), 1) * tokens).astype(jnp.float32)
    for s in range(blocks):
        if s < rank_slots:
            block_id = me * rank_slots + s
            for b in range(chips * chip_blocks):
                block_id = jnp.where(spill[b] == me * rank_slots + s, -1, block_id)
        else:
            block_id = spill[me * per_rank + s - rank_slots]
        bound = jnp.max(jnp.where(owned == block_id, after, float(-FAR)), axis=1, keepdims=True)
        bias[:, pl.ds(s * tokens, tokens)] = jnp.where(edge < bound, 0.0, LOW).astype(jnp.float32)
    lse[...] = jnp.zeros_like(lse)

    load_kp.wait()
    load_vp.wait()
    load_kc.wait()
    load_vc.wait()
    q_copy.wait()

    attending = KV // HEADS_PER_STEP

    def mixed(i, carry):
        near_step(i)
        far_step(i - 1)
        for e in range(HEADS_PER_STEP):
            attend((i - 1) * HEADS_PER_STEP + e)
        return carry

    lax.fori_loop(1, 1 + attending, mixed, 0)

    theirs = pl.ds((1 - core) * chips, chips)
    s1_o = remote(part.at[theirs], pin_o, s1_s.at[0], s1_r.at[0], partner)
    s1_l = remote(lse.at[theirs], pin_l, s1_s.at[1], s1_r.at[1], partner)
    s1_o.start()
    s1_l.start()
    near_step(1 + attending)
    s1_o.wait_recv()
    s1_l.wait_recv()

    level_a, level_b = lse[ours], pin_l[...]
    top = jnp.maximum(level_a, level_b)
    ea, eb = jnp.exp(level_a - top), jnp.exp(level_b - top)
    both = ea + eb
    ml[...] = top + jnp.log(both)
    wa, wb = ea / both, eb / both
    for h in range(KV):
        mixed_rows = part[ours, h] * wa[:, :, h : h + 1] + pin_o[:, h] * wb[:, :, h : h + 1]
        mo[:, h] = mixed_rows.astype(jnp.bfloat16)
    s2 = []
    for off in range(1, chips):
        to = lax.rem(z + off, chips)
        s2.append(remote(mo.at[to], ro.at[z], s2_s.at[0, off], s2_r.at[0, z], 2 * to + core))
        s2.append(remote(ml.at[to], rl.at[z], s2_s.at[1, off], s2_r.at[1, z], 2 * to + core))
    for copy in s2:
        copy.start()
    ro[z] = mo[z]
    rl[z] = ml[z]
    far_step(attending)

    def moving(i, carry):
        near_step(i)
        far_step(i - 1)
        return carry

    if lanes > 2 + attending:
        lax.fori_loop(2 + attending, lanes, moving, 0)
    if lanes > 1 + attending:
        far_step(lanes - 1)

    @pl.when(far == chips - 1)
    def _():
        def drain(i, carry):
            for p in range(PIECES):
                lane_copy(far_way, lanes - 1 - i, p, far_next).wait_recv()
            return carry

        lax.fori_loop(0, lanes, drain, 0)

    def gathered(b, q, target):
        at_home = lax.div(b, jnp.int32(chip_blocks)) == z
        index = jnp.clip(b - z * chip_blocks, 0, chip_blocks - 1)
        way_of, lane_of = jnp.int32(0), jnp.int32(0)
        for way in range(2):
            for l in range(lanes):
                hit = arrivals[way][l] == b
                way_of = jnp.where(hit, way, way_of)
                lane_of = jnp.where(hit, l, lane_of)
        target[q] = lax.select(at_home, own[index], arr[way_of, lane_of])

    for q, b in enumerate(blocks_for(partner, rank_of, per_rank)):
        gathered(b, q, pout)
    handed = remote(pout, newk, fx_s, fx_r, partner)

    @pl.when(core == 0)
    def _():
        handed.start()

    @pl.when(core == 1)
    def _():
        remote(pout, newv, fx_s, fx_r, partner).start()

    for q, b in enumerate(blocks_for(me, rank_of, per_rank)):
        gathered(b, q, fin)

    @pl.when(core == 0)
    def _():
        pltpu.make_async_copy(fin, newk, out_s).start()

    @pl.when(core == 1)
    def _():
        pltpu.make_async_copy(fin, newv, out_s).start()

    for off in range(1, chips):
        source = lax.rem(z + off, chips)
        remote(mo.at[source], ro.at[source], s2_s.at[0, off], s2_r.at[0, source], partner).wait_recv()
        remote(ml.at[source], rl.at[source], s2_s.at[1, off], s2_r.at[1, source], partner).wait_recv()
    levels = rl[...]
    top = jnp.max(levels, axis=0, keepdims=True)
    shares = jnp.exp(levels - top)
    shares = shares / jnp.sum(shares, axis=0, keepdims=True)
    for h in range(KV):
        rows = jnp.sum(ro[:, h].astype(jnp.float32) * shares[:, :, h : h + 1], axis=0)
        for j in range(GROUPS * rows_here):
            head = h * GROUPS + j // rows_here
            i = j % rows_here
            att_wide[i : i + 1, head * HEAD : (head + 1) * HEAD] = rows[j : j + 1, :]
    att[...] = att_wide[...].astype(jnp.bfloat16)

    handed.wait_recv()

    handed.wait_send()
    s1_o.wait_send()
    s1_l.wait_send()
    for copy in s2:
        copy.wait_send()
    for l in range(2):
        @pl.when(l < chip_blocks * (near + 1))
        def _():
            for p in range(PIECES):
                lane_copy(near_way, l, p, near_next).wait_send()

    @pl.when(far < chips - 1)
    def _():
        def sent(i, carry):
            for p in range(PIECES):
                lane_copy(far_way, i, p, far_next).wait_send()
            return carry

        lax.fori_loop(0, lanes, sent, 0)

    pltpu.make_async_copy(fin, newk, out_s).wait()


def load_kernel(
    chips, chip_blocks, rank_slots, steps, spill, q_in, pk, pv, pick, qg, other,
    box, q_wide, q_ref, send, recv, q_s, q_r, ex_s, ex_r,
):
    groups = lax.axis_size("grp")
    mine = lax.axis_index("grp")
    me = lax.axis_index("blk")
    z = me // 2
    core = lax.rem(me, 2)
    partner = 2 * z + 1 - core
    rows_here = q_in.shape[0]
    barrier = pltpu.get_barrier_semaphore()
    pl.semaphore_signal(barrier, inc=1, device_id={"blk": partner}, device_id_type=MESH)
    for off in range(1, groups):
        pl.semaphore_signal(barrier, inc=1, device_id={"grp": lax.rem(mine + off, groups)}, device_id_type=MESH)
    for off in range(1, chips):
        peer = 2 * lax.rem(z + off, chips) + core
        pl.semaphore_signal(barrier, inc=1, device_id={"blk": peer}, device_id_type=MESH)

    chip_of = [lax.div(spill[b], jnp.int32(2 * rank_slots)) for b in range(chips * chip_blocks)]
    load = jnp.int32(0)
    for n in range(chips - 1):
        crossing = jnp.int32(0)
        for b in range((n + 1) * chip_blocks):
            crossing = crossing + (chip_of[b] > n).astype(jnp.int32)
        load = jnp.maximum(load, crossing)
    box[mine] = jnp.full(box.shape[1:], load, jnp.int32)
    q_wide[...] = jnp.zeros_like(q_wide)
    q_rows = q_in[...].astype(jnp.float32)
    for h in range(KV):
        for j in range(GROUPS * rows_here):
            head = h * GROUPS + j // rows_here
            i = j % rows_here
            q_wide[h, j : j + 1, :] = q_rows[i : i + 1, head * HEAD : (head + 1) * HEAD]
    q_ref[...] = q_wide[...].astype(jnp.bfloat16)
    pl.semaphore_wait(barrier, groups + chips - 1)

    def copy_to(off, source):
        return pltpu.make_async_remote_copy(
            src_ref=box.at[mine], dst_ref=box.at[mine], send_sem=send.at[off], recv_sem=recv.at[source],
            device_id={"grp": lax.rem(mine + off, groups)}, device_id_type=MESH,
        )

    def remote(src, dst, s, r, rank):
        return pltpu.make_async_remote_copy(
            src_ref=src, dst_ref=dst, send_sem=s, recv_sem=r, device_id={"blk": rank}, device_id_type=MESH
        )

    for off in range(1, groups):
        copy_to(off, mine).start()
    q_copies = []
    for off in range(1, chips):
        peer = 2 * lax.rem(z + off, chips) + core
        q_copies.append(remote(q_ref, qg.at[z], q_s.at[off], q_r.at[z], peer))
    for copy in q_copies:
        copy.start()

    @pl.when(core == 0)
    def _():
        remote(pv, other, ex_s, ex_r, partner).start()

    @pl.when(core == 1)
    def _():
        remote(pk, other, ex_s, ex_r, partner).start()

    qg[z] = q_ref[...]
    for off in range(1, groups):
        copy_to(off, lax.rem(mine + off, groups)).wait_recv()
    largest = jnp.max(box[...])
    choice = jnp.int32(0)
    for step in steps[:-1]:
        choice = choice + (largest > step).astype(jnp.int32)
    pick[0] = choice
    for off in range(1, chips):
        came = lax.rem(z + off, chips)
        remote(q_ref, qg.at[came], q_s.at[off], q_r.at[came], partner).wait_recv()
    exchanged = remote(pk, other, ex_s, ex_r, partner)
    exchanged.wait_recv()
    exchanged.wait_send()
    for copy in q_copies:
        copy.wait_send()
    for off in range(1, groups):
        copy_to(off, mine).wait_send()


def place_kernel(spill, first_ref, ck, cv, newk, newv, att_in, pool_k, pool_v, att_out, hold, into, out):
    rank_slots = ck.shape[0]
    first = first_ref[0]
    filled = [jnp.bool_(False)] * rank_slots
    count = jnp.int32(0)
    for b in range(spill.shape[0]):
        at = spill[b] - first
        mine = (at >= 0) & (at < rank_slots)
        filled = [filled[j] | (at == j) for j in range(rank_slots)]
        here, which = jnp.clip(at, 0, rank_slots - 1), jnp.minimum(count, newk.shape[0] - 1)

        @pl.when(mine)
        def _():
            pltpu.make_async_copy(newk.at[which], hold.at[0, here], into.at[0, here]).start()
            pltpu.make_async_copy(newv.at[which], hold.at[1, here], into.at[1, here]).start()

        count = count + mine.astype(jnp.int32)
    for j in range(rank_slots):
        @pl.when(jnp.logical_not(filled[j]))
        def _():
            pltpu.make_async_copy(ck.at[j], hold.at[0, j], into.at[0, j]).start()
            pltpu.make_async_copy(cv.at[j], hold.at[1, j], into.at[1, j]).start()

    att_out[...] = att_in[...]
    stores = []
    for j in range(rank_slots):
        for t, (source, target) in enumerate(((ck, pool_k), (cv, pool_v))):
            pltpu.make_async_copy(source.at[j], hold.at[t, j], into.at[t, j]).wait()
            stores.append(pltpu.make_async_copy(hold.at[t, j], target.at[j], out.at[t, j]))
            stores[-1].start()
    for copy in stores:
        copy.wait()


def per_device(
    queries, cache_keys, pool_values_prior, prefill_keys, prefill_values, context_lengths, block_table, spill_slots
):
    ranks = lax.axis_size("blk")
    chips = ranks // 2
    me = lax.axis_index("blk")
    rank_slots, tokens, width = cache_keys.shape
    per_rank = prefill_keys.shape[0]
    chip_blocks = 2 * per_rank
    blocks = rank_slots + per_rank
    most = chip_blocks * (chips // 2)
    choices = (most // 2, most * 5 // 8, most * 3 // 4, most)
    rows_here, query_width = queries.shape
    first = me * rank_slots

    bf, f32 = jnp.bfloat16, jnp.float32
    vmem = pltpu.VMEM
    dma = pltpu.SemaphoreType.DMA
    any_spec = pl.BlockSpec(memory_space=pl.ANY)
    smem_spec = pl.BlockSpec(memory_space=pltpu.SMEM)
    vmem_spec = pl.BlockSpec(memory_space=pltpu.VMEM)
    block = (tokens, width)
    def exchange(number, lanes, *operands):
        return pl.pallas_call(
            functools.partial(exchange_kernel, chips, lanes),
            out_shape=(
                jax.ShapeDtypeStruct(queries.shape, bf),
                jax.ShapeDtypeStruct((per_rank, *block), bf),
                jax.ShapeDtypeStruct((per_rank, *block), bf),
            ),
            in_specs=[smem_spec, vmem_spec, smem_spec, vmem_spec] + [any_spec] * 5,
            out_specs=(vmem_spec, any_spec, any_spec),
            scratch_shapes=[
                vmem((blocks, *block), bf),
                vmem((blocks, *block), bf),
                vmem((chip_blocks, *block), bf),
                vmem((2, lanes, *block), bf),
                vmem((2, lanes, *block), bf),
                vmem((per_rank, *block), bf),
                vmem((per_rank, *block), bf),
                vmem((ranks, KV, ROWS, HEAD), bf),
                vmem((ranks * ROWS, blocks * tokens), f32),
                vmem((ranks, KV, ROWS, HEAD), f32),
                vmem((ranks, ROWS, HEAD), f32),
                vmem((chips, KV, ROWS, HEAD), f32),
                vmem((chips, ROWS, HEAD), f32),
                vmem((chips, KV, ROWS, HEAD), bf),
                vmem((chips, ROWS, HEAD), f32),
                vmem((chips, KV, ROWS, HEAD), bf),
                vmem((chips, ROWS, HEAD), f32),
                pltpu.SMEM((2, lanes), jnp.int32),
                vmem(queries.shape, f32),
                dma((6,)),
                dma,
                dma,
                dma((2, lanes, PIECES)),
                dma((2, lanes, PIECES)),
                dma((2,)),
                dma((2,)),
                dma((2, chips)),
                dma((2, chips)),
                dma,
                dma,
                dma,
            ],
            compiler_params=pltpu.CompilerParams(
                collective_id=1 + number, has_side_effects=True, vmem_limit_bytes=VMEM_BYTES
            ),
            name="exchange",
        )(*operands)

    pick, gathered_queries, other = pl.pallas_call(
        functools.partial(load_kernel, chips, chip_blocks, rank_slots, choices),
        out_shape=(
            jax.ShapeDtypeStruct((1,), jnp.int32),
            jax.ShapeDtypeStruct((chips, KV, ROWS, HEAD), bf),
            jax.ShapeDtypeStruct((per_rank, *block), bf),
        ),
        in_specs=[smem_spec, vmem_spec, any_spec, any_spec],
        out_specs=(smem_spec, vmem_spec, vmem_spec),
        scratch_shapes=[
            vmem((lax.axis_size("grp"), 8, HEAD), jnp.int32),
            vmem((KV, ROWS, HEAD), f32),
            vmem((KV, ROWS, HEAD), bf),
            dma((lax.axis_size("grp"),)),
            dma((lax.axis_size("grp"),)),
            dma((chips,)),
            dma((chips,)),
            dma,
            dma,
        ],
        compiler_params=pltpu.CompilerParams(
            collective_id=0, has_side_effects=True, vmem_limit_bytes=VMEM_BYTES
        ),
        name="load",
    )(spill_slots, queries, prefill_keys, prefill_values)
    att, newk, newv = lax.switch(
        pick[0],
        [functools.partial(exchange, number, lanes) for number, lanes in enumerate(choices)],
        context_lengths, block_table, spill_slots, gathered_queries, other,
        prefill_keys, prefill_values, cache_keys, pool_values_prior,
    )

    pool_keys, pool_values, att = pl.pallas_call(
        place_kernel,
        out_shape=(
            jax.ShapeDtypeStruct(cache_keys.shape, bf),
            jax.ShapeDtypeStruct(cache_keys.shape, bf),
            jax.ShapeDtypeStruct(att.shape, bf),
        ),
        in_specs=[smem_spec, smem_spec] + [any_spec] * 4 + [vmem_spec],
        out_specs=(any_spec, any_spec, vmem_spec),
        scratch_shapes=[vmem((2, rank_slots, *block), bf), dma((2, rank_slots)), dma((2, rank_slots))],
        compiler_params=pltpu.CompilerParams(vmem_limit_bytes=VMEM_BYTES),
        name="place",
    )(spill_slots, first.reshape(1), cache_keys, pool_values_prior, newk, newv, att)
    return att, pool_keys, pool_values


def solution(mesh):
    both = ("grp", "blk")
    return jax.shard_map(
        per_device,
        mesh=mesh,
        in_specs=(P(both, None),) + (P(both, None, None),) * 4 + (P("grp"), P("grp", None), P("grp")),
        out_specs=(P(both, None), P(both, None, None), P(both, None, None)),
        check_vma=False,
    )
```

```python
import functools

import jax
import jax.numpy as jnp
from jax import lax
from jax.experimental import pallas as pl
from jax.experimental.pallas import tpu as pltpu
from jax.sharding import PartitionSpec as P

QUERY_HEADS = 40
KV = 8
GROUPS = QUERY_HEADS // KV
HEAD = 128
STEPS = 4
REQ = 4
ROWS = 16
PIECES = 4
HEADS_PER_STEP = 2
LOW = -1e30
FAR = 1 << 24
VMEM_BYTES = 60 * 1024 * 1024
MESH = pl.DeviceIdType.MESH


def lane_plan(spill, chips, z, lanes, chip_blocks, rank_slots):
    total = chips * chip_blocks
    rank_of = [lax.div(spill[b], jnp.int32(rank_slots)) for b in range(total)]
    chip_of = [r >> 1 for r in rank_of]
    sends, arrivals = [], []
    for way in range(2):
        dest = chip_of if way == 0 else [chips - 1 - c for c in chip_of]
        place = z if way == 0 else chips - 1 - z
        lane_dest = [jnp.int32(-1)] * lanes
        lane_block = [jnp.int32(-1)] * lanes
        send = [jnp.int32(chip_blocks)] * lanes
        arrive = [jnp.int32(-1)] * lanes
        for n in range(chips):
            here = place == n
            if n > 0:
                arrive = [jnp.where(here, lane_block[l], arrive[l]) for l in range(lanes)]
            if n == chips - 1:
                break
            first = (n if way == 0 else chips - 1 - n) * chip_blocks
            left = [dest[first + i] > n for i in range(chip_blocks)]
            for l in reversed(range(min(lanes, chip_blocks * (n + 1)))):
                pick, pick_dest = jnp.int32(chip_blocks), jnp.int32(-1)
                for i in reversed(range(chip_blocks)):
                    pick = jnp.where(left[i], i, pick)
                    pick_dest = jnp.where(left[i], dest[first + i], pick_dest)
                take = (lane_dest[l] <= n) & (pick < chip_blocks)
                left = [left[i] & jnp.logical_not(take & (pick == i)) for i in range(chip_blocks)]
                lane_dest[l] = jnp.where(take, pick_dest, lane_dest[l])
                lane_block[l] = jnp.where(take, first + pick, lane_block[l])
                send[l] = jnp.where(here & take, pick, send[l])
        sends.append(send)
        arrivals.append(arrive)
    return rank_of, sends, arrivals


def blocks_for(rank, rank_of, per_rank):
    found = [jnp.int32(0)] * per_rank
    count = jnp.int32(0)
    for b, target in enumerate(rank_of):
        hit = target == rank
        found = [jnp.where(hit & (count == q), b, found[q]) for q in range(per_rank)]
        count = count + hit.astype(jnp.int32)
    return found


def exchange_kernel(
    chips, lanes, lengths, table, spill, q_half, other, pk, pv, ck, cv,
    att, newk, newv,
    kall, vall, own, arr, snd, fin, pout, qg, bias, part, lse, pin_o, pin_l, mo, ml, ro, rl, sched, att_wide,
    loc, q_s, q_r, lane_s, lane_r, s1_s, s1_r, s2_s, s2_r, fx_s, fx_r, out_s,
):
    rank_slots, tokens, width = ck.shape
    per_rank = pk.shape[0]
    chip_blocks = 2 * per_rank
    blocks = rank_slots + per_rank
    rows_here = STEPS * REQ // (2 * chips)
    piece = tokens // PIECES
    me = lax.axis_index("blk")
    z = me // 2
    core = lax.rem(me, 2)
    partner = 2 * z + 1 - core

    def remote(src, dst, s, r, rank):
        return pltpu.make_async_remote_copy(
            src_ref=src, dst_ref=dst, send_sem=s, recv_sem=r, device_id={"blk": rank}, device_id_type=MESH
        )

    load_kp = pltpu.make_async_copy(pk, kall.at[pl.ds(rank_slots, per_rank)], loc.at[0])
    load_vp = pltpu.make_async_copy(pv, vall.at[pl.ds(rank_slots, per_rank)], loc.at[1])
    load_kc = pltpu.make_async_copy(ck, kall.at[pl.ds(0, rank_slots)], loc.at[2])
    load_vc = pltpu.make_async_copy(cv, vall.at[pl.ds(0, rank_slots)], loc.at[3])
    own_mine = own.at[pl.ds(core * per_rank, per_rank)]

    @pl.when(core == 0)
    def _():
        pltpu.make_async_copy(pk, own_mine, loc.at[4]).start()

    @pl.when(core == 1)
    def _():
        pltpu.make_async_copy(pv, own_mine, loc.at[4]).start()

    load_other = pltpu.make_async_copy(other, own.at[pl.ds((1 - core) * per_rank, per_rank)], loc.at[5])
    load_other.start()
    load_kp.start()
    load_vp.start()
    load_kc.start()
    load_vc.start()

    barrier = pltpu.get_barrier_semaphore()
    pl.semaphore_signal(barrier, inc=1, device_id={"blk": partner}, device_id_type=MESH)
    for off in range(1, chips):
        peer = 2 * lax.rem(z + off, chips) + core
        pl.semaphore_signal(barrier, inc=1, device_id={"blk": peer}, device_id_type=MESH)
    rank_of, sends, arrivals = lane_plan(spill, chips, z, lanes, chip_blocks, rank_slots)
    for way in range(2):
        for l in range(lanes):
            sched[way, l] = sends[way][l]
    pltpu.make_async_copy(pk, own_mine, loc.at[4]).wait()
    load_other.wait()
    pl.semaphore_wait(barrier, chips)
    ours = pl.ds(core * chips, chips)
    q_copy = remote(q_half, qg.at[ours], q_s, q_r, partner)
    q_copy.start()

    low_half = z < chips // 2
    near = jnp.where(low_half, z, chips - 1 - z)
    far = chips - 1 - near
    near_way = jnp.where(low_half, 0, 1)
    far_way = 1 - near_way
    near_next = 2 * jnp.where(low_half, z + 1, z - 1) + core
    far_next = 2 * jnp.where(low_half, jnp.maximum(z - 1, 0), jnp.minimum(z + 1, chips - 1)) + core

    def lane_copy(way, l, p, rank):
        rows = pl.ds(p * piece, piece)
        return remote(
            snd.at[way, l, rows], arr.at[way, l, rows], lane_s.at[way, l, p], lane_r.at[way, l, p], rank
        )

    def compose(way, l, p):
        rows = pl.ds(p * piece, piece)
        pick = sched[way, l]
        snd[way, l, rows] = lax.select(
            pick == chip_blocks, arr[way, l, rows], own[jnp.minimum(pick, chip_blocks - 1), rows]
        )

    def compose_own(way, l, p):
        rows = pl.ds(p * piece, piece)
        snd[way, l, rows] = own[jnp.minimum(sched[way, l], chip_blocks - 1), rows]

    def near_step(i):
        l = lanes - 1 - i
        if isinstance(i, int) and l < 0:
            return
        passing = (l >= 0) & (l < chip_blocks * near)
        starting = (l >= 0) & jnp.logical_not(passing) & (l < chip_blocks * (near + 1))

        @pl.when((l >= 0) & (l + 2 < lanes) & (l + 2 < chip_blocks * (near + 1)))
        def _():
            for p in range(PIECES):
                lane_copy(near_way, l + 2, p, near_next).wait_send()

        @pl.when(passing)
        def _():
            for p in range(PIECES):
                lane_copy(near_way, l, p, near_next).wait_recv()
                compose(near_way, l, p)
                lane_copy(near_way, l, p, near_next).start()

        @pl.when(starting)
        def _():
            for p in range(PIECES):
                compose_own(near_way, l, p)
                lane_copy(near_way, l, p, near_next).start()

    def far_step(i):
        l = lanes - 1 - i
        if isinstance(i, int) and l < 0:
            return

        @pl.when((l >= 0) & (far < chips - 1))
        def _():
            for p in range(PIECES):
                lane_copy(far_way, l, p, far_next).wait_recv()
                compose(far_way, l, p)
                lane_copy(far_way, l, p, far_next).start()

    def attend(h):
        cols = pl.ds(pl.multiple_of(h * HEAD, HEAD), HEAD)
        q = qg[:, h].reshape(2 * chips * ROWS, HEAD)
        k = kall[:, :, cols].reshape(blocks * tokens, HEAD)
        v = vall[:, :, cols].reshape(blocks * tokens, HEAD)
        s = lax.dot_general(q, k, (((1,), (1,)), ((), ())), preferred_element_type=jnp.float32)
        s = s * HEAD ** (-0.5) + bias[...]
        m = jnp.max(s, axis=1, keepdims=True)
        w = jnp.exp(s - m)
        total = jnp.sum(w, axis=1, keepdims=True)
        o = jnp.dot(w.astype(jnp.bfloat16), v, preferred_element_type=jnp.float32) / total
        part[:, h] = o.reshape(2 * chips, ROWS, HEAD)
        lane = lax.broadcasted_iota(jnp.int32, (2 * chips, ROWS, HEAD), 2)
        level = (m + jnp.log(total)).reshape(2 * chips, ROWS, 1)
        lse[...] = jnp.where(lane == h, level, lse[...])

    near_step(0)
    qg[ours] = q_half[...]

    row_count = 2 * chips * ROWS
    row = lax.broadcasted_iota(jnp.int32, (row_count, HEAD), 0)
    slot, inner = row >> (ROWS.bit_length() - 1), row & (ROWS - 1)
    rank_row = 2 * (slot & (chips - 1)) + (slot >> (chips.bit_length() - 1))
    row_id = rank_row * rows_here + (inner & (rows_here - 1))
    valid = inner < GROUPS * rows_here
    step, request = row_id >> (REQ.bit_length() - 1), row_id & (REQ - 1)
    token = lax.broadcasted_iota(jnp.int32, (row_count, HEAD), 1)
    edge = jnp.where(valid, token + (STEPS - 1) - step, FAR).astype(jnp.float32)
    columns = table.shape[1]
    owned = jnp.broadcast_to(table[0:1, :], (row_count, columns))
    length = jnp.full((row_count, columns), lengths[0], jnp.int32)
    for r in range(1, REQ):
        here = request[:, :columns] == r
        owned = jnp.where(here, table[r : r + 1, :], owned)
        length = jnp.where(here, lengths[r], length)
    after = (length - lax.broadcasted_iota(jnp.int32, (row_count, columns), 1) * tokens).astype(jnp.float32)
    for s in range(blocks):
        if s < rank_slots:
            block_id = me * rank_slots + s
            for b in range(chips * chip_blocks):
                block_id = jnp.where(spill[b] == me * rank_slots + s, -1, block_id)
        else:
            block_id = spill[me * per_rank + s - rank_slots]
        bound = jnp.max(jnp.where(owned == block_id, after, float(-FAR)), axis=1, keepdims=True)
        bias[:, pl.ds(s * tokens, tokens)] = jnp.where(edge < bound, 0.0, LOW).astype(jnp.float32)
    lse[...] = jnp.zeros_like(lse)

    load_kp.wait()
    load_vp.wait()
    load_kc.wait()
    load_vc.wait()
    q_copy.wait()

    attending = KV // HEADS_PER_STEP

    def mixed(i, carry):
        near_step(i)
        far_step(i - 1)
        for e in range(HEADS_PER_STEP):
            attend((i - 1) * HEADS_PER_STEP + e)
        return carry

    lax.fori_loop(1, 1 + attending, mixed, 0)

    theirs = pl.ds((1 - core) * chips, chips)
    s1_o = remote(part.at[theirs], pin_o, s1_s.at[0], s1_r.at[0], partner)
    s1_l = remote(lse.at[theirs], pin_l, s1_s.at[1], s1_r.at[1], partner)
    s1_o.start()
    s1_l.start()
    near_step(1 + attending)
    s1_o.wait_recv()
    s1_l.wait_recv()

    level_a, level_b = lse[ours], pin_l[...]
    top = jnp.maximum(level_a, level_b)
    ea, eb = jnp.exp(level_a - top), jnp.exp(level_b - top)
    both = ea + eb
    ml[...] = top + jnp.log(both)
    wa, wb = ea / both, eb / both
    for h in range(KV):
        mixed_rows = part[ours, h] * wa[:, :, h : h + 1] + pin_o[:, h] * wb[:, :, h : h + 1]
        mo[:, h] = mixed_rows.astype(jnp.bfloat16)
    s2 = []
    for off in range(1, chips):
        to = lax.rem(z + off, chips)
        s2.append(remote(mo.at[to], ro.at[z], s2_s.at[0, off], s2_r.at[0, z], 2 * to + core))
        s2.append(remote(ml.at[to], rl.at[z], s2_s.at[1, off], s2_r.at[1, z], 2 * to + core))
    for copy in s2:
        copy.start()
    ro[z] = mo[z]
    rl[z] = ml[z]
    far_step(attending)

    def moving(i, carry):
        near_step(i)
        far_step(i - 1)
        return carry

    if lanes > 2 + attending:
        lax.fori_loop(2 + attending, lanes, moving, 0)
    if lanes > 1 + attending:
        far_step(lanes - 1)

    @pl.when(far == chips - 1)
    def _():
        def drain(i, carry):
            for p in range(PIECES):
                lane_copy(far_way, lanes - 1 - i, p, far_next).wait_recv()
            return carry

        lax.fori_loop(0, lanes, drain, 0)

    def gathered(b, q, target):
        at_home = lax.div(b, jnp.int32(chip_blocks)) == z
        index = jnp.clip(b - z * chip_blocks, 0, chip_blocks - 1)
        way_of, lane_of = jnp.int32(0), jnp.int32(0)
        for way in range(2):
            for l in range(lanes):
                hit = arrivals[way][l] == b
                way_of = jnp.where(hit, way, way_of)
                lane_of = jnp.where(hit, l, lane_of)
        target[q] = lax.select(at_home, own[index], arr[way_of, lane_of])

    for q, b in enumerate(blocks_for(partner, rank_of, per_rank)):
        gathered(b, q, pout)
    handed = remote(pout, newk, fx_s, fx_r, partner)

    @pl.when(core == 0)
    def _():
        handed.start()

    @pl.when(core == 1)
    def _():
        remote(pout, newv, fx_s, fx_r, partner).start()

    for q, b in enumerate(blocks_for(me, rank_of, per_rank)):
        gathered(b, q, fin)

    @pl.when(core == 0)
    def _():
        pltpu.make_async_copy(fin, newk, out_s).start()

    @pl.when(core == 1)
    def _():
        pltpu.make_async_copy(fin, newv, out_s).start()

    for off in range(1, chips):
        source = lax.rem(z + off, chips)
        remote(mo.at[source], ro.at[source], s2_s.at[0, off], s2_r.at[0, source], partner).wait_recv()
        remote(ml.at[source], rl.at[source], s2_s.at[1, off], s2_r.at[1, source], partner).wait_recv()
    levels = rl[...]
    top = jnp.max(levels, axis=0, keepdims=True)
    shares = jnp.exp(levels - top)
    shares = shares / jnp.sum(shares, axis=0, keepdims=True)
    for h in range(KV):
        rows = jnp.sum(ro[:, h].astype(jnp.float32) * shares[:, :, h : h + 1], axis=0)
        for j in range(GROUPS * rows_here):
            head = h * GROUPS + j // rows_here
            i = j % rows_here
            att_wide[i : i + 1, head * HEAD : (head + 1) * HEAD] = rows[j : j + 1, :]
    att[...] = att_wide[...].astype(jnp.bfloat16)

    handed.wait_recv()

    handed.wait_send()
    s1_o.wait_send()
    s1_l.wait_send()
    for copy in s2:
        copy.wait_send()
    for l in range(2):
        @pl.when(l < chip_blocks * (near + 1))
        def _():
            for p in range(PIECES):
                lane_copy(near_way, l, p, near_next).wait_send()

    @pl.when(far < chips - 1)
    def _():
        def sent(i, carry):
            for p in range(PIECES):
                lane_copy(far_way, i, p, far_next).wait_send()
            return carry

        lax.fori_loop(0, lanes, sent, 0)

    pltpu.make_async_copy(fin, newk, out_s).wait()


def load_kernel(
    chips, chip_blocks, rank_slots, steps, spill, q_in, pk, pv, pick, qg, other,
    box, q_wide, q_ref, send, recv, q_s, q_r, ex_s, ex_r,
):
    groups = lax.axis_size("grp")
    mine = lax.axis_index("grp")
    me = lax.axis_index("blk")
    z = me // 2
    core = lax.rem(me, 2)
    partner = 2 * z + 1 - core
    rows_here = q_in.shape[0]
    barrier = pltpu.get_barrier_semaphore()
    pl.semaphore_signal(barrier, inc=1, device_id={"blk": partner}, device_id_type=MESH)
    for off in range(1, groups):
        pl.semaphore_signal(barrier, inc=1, device_id={"grp": lax.rem(mine + off, groups)}, device_id_type=MESH)
    for off in range(1, chips):
        peer = 2 * lax.rem(z + off, chips) + core
        pl.semaphore_signal(barrier, inc=1, device_id={"blk": peer}, device_id_type=MESH)

    chip_of = [lax.div(spill[b], jnp.int32(2 * rank_slots)) for b in range(chips * chip_blocks)]
    load = jnp.int32(0)
    for n in range(chips - 1):
        crossing = jnp.int32(0)
        for b in range((n + 1) * chip_blocks):
            crossing = crossing + (chip_of[b] > n).astype(jnp.int32)
        load = jnp.maximum(load, crossing)
    box[mine] = jnp.full(box.shape[1:], load, jnp.int32)
    q_wide[...] = jnp.zeros_like(q_wide)
    q_rows = q_in[...].astype(jnp.float32)
    for h in range(KV):
        for j in range(GROUPS * rows_here):
            head = h * GROUPS + j // rows_here
            i = j % rows_here
            q_wide[h, j : j + 1, :] = q_rows[i : i + 1, head * HEAD : (head + 1) * HEAD]
    q_ref[...] = q_wide[...].astype(jnp.bfloat16)
    pl.semaphore_wait(barrier, groups + chips - 1)

    def copy_to(off, source):
        return pltpu.make_async_remote_copy(
            src_ref=box.at[mine], dst_ref=box.at[mine], send_sem=send.at[off], recv_sem=recv.at[source],
            device_id={"grp": lax.rem(mine + off, groups)}, device_id_type=MESH,
        )

    def remote(src, dst, s, r, rank):
        return pltpu.make_async_remote_copy(
            src_ref=src, dst_ref=dst, send_sem=s, recv_sem=r, device_id={"blk": rank}, device_id_type=MESH
        )

    for off in range(1, groups):
        copy_to(off, mine).start()
    q_copies = []
    for off in range(1, chips):
        peer = 2 * lax.rem(z + off, chips) + core
        q_copies.append(remote(q_ref, qg.at[z], q_s.at[off], q_r.at[z], peer))
    for copy in q_copies:
        copy.start()

    @pl.when(core == 0)
    def _():
        remote(pv, other, ex_s, ex_r, partner).start()

    @pl.when(core == 1)
    def _():
        remote(pk, other, ex_s, ex_r, partner).start()

    qg[z] = q_ref[...]
    for off in range(1, groups):
        copy_to(off, lax.rem(mine + off, groups)).wait_recv()
    largest = jnp.max(box[...])
    choice = jnp.int32(0)
    for step in steps[:-1]:
        choice = choice + (largest > step).astype(jnp.int32)
    pick[0] = choice
    for off in range(1, chips):
        came = lax.rem(z + off, chips)
        remote(q_ref, qg.at[came], q_s.at[off], q_r.at[came], partner).wait_recv()
    exchanged = remote(pk, other, ex_s, ex_r, partner)
    exchanged.wait_recv()
    exchanged.wait_send()
    for copy in q_copies:
        copy.wait_send()
    for off in range(1, groups):
        copy_to(off, mine).wait_send()


def place_kernel(spill, first_ref, ck, cv, newk, newv, att_in, pool_k, pool_v, att_out, hold, into, out):
    rank_slots = ck.shape[0]
    first = first_ref[0]
    filled = [jnp.bool_(False)] * rank_slots
    count = jnp.int32(0)
    for b in range(spill.shape[0]):
        at = spill[b] - first
        mine = (at >= 0) & (at < rank_slots)
        filled = [filled[j] | (at == j) for j in range(rank_slots)]
        here, which = jnp.clip(at, 0, rank_slots - 1), jnp.minimum(count, newk.shape[0] - 1)

        @pl.when(mine)
        def _():
            pltpu.make_async_copy(newk.at[which], hold.at[0, here], into.at[0, here]).start()
            pltpu.make_async_copy(newv.at[which], hold.at[1, here], into.at[1, here]).start()

        count = count + mine.astype(jnp.int32)
    for j in range(rank_slots):
        @pl.when(jnp.logical_not(filled[j]))
        def _():
            pltpu.make_async_copy(ck.at[j], hold.at[0, j], into.at[0, j]).start()
            pltpu.make_async_copy(cv.at[j], hold.at[1, j], into.at[1, j]).start()

    att_out[...] = att_in[...]
    stores = []
    for j in range(rank_slots):
        for t, (source, target) in enumerate(((ck, pool_k), (cv, pool_v))):
            pltpu.make_async_copy(source.at[j], hold.at[t, j], into.at[t, j]).wait()
            stores.append(pltpu.make_async_copy(hold.at[t, j], target.at[j], out.at[t, j]))
            stores[-1].start()
    for copy in stores:
        copy.wait()


def per_device(
    queries, cache_keys, pool_values_prior, prefill_keys, prefill_values, context_lengths, block_table, spill_slots
):
    ranks = lax.axis_size("blk")
    chips = ranks // 2
    me = lax.axis_index("blk")
    rank_slots, tokens, width = cache_keys.shape
    per_rank = prefill_keys.shape[0]
    chip_blocks = 2 * per_rank
    blocks = rank_slots + per_rank
    most = chip_blocks * (chips // 2)
    choices = (most // 2, most * 5 // 8, most * 3 // 4, most)
    rows_here, query_width = queries.shape
    first = me * rank_slots

    bf, f32 = jnp.bfloat16, jnp.float32
    vmem = pltpu.VMEM
    dma = pltpu.SemaphoreType.DMA
    any_spec = pl.BlockSpec(memory_space=pl.ANY)
    smem_spec = pl.BlockSpec(memory_space=pltpu.SMEM)
    vmem_spec = pl.BlockSpec(memory_space=pltpu.VMEM)
    block = (tokens, width)
    def exchange(number, lanes, *operands):
        return pl.pallas_call(
            functools.partial(exchange_kernel, chips, lanes),
            out_shape=(
                jax.ShapeDtypeStruct(queries.shape, bf),
                jax.ShapeDtypeStruct((per_rank, *block), bf),
                jax.ShapeDtypeStruct((per_rank, *block), bf),
            ),
            in_specs=[smem_spec, vmem_spec, smem_spec, vmem_spec] + [any_spec] * 5,
            out_specs=(vmem_spec, any_spec, any_spec),
            scratch_shapes=[
                vmem((blocks, *block), bf),
                vmem((blocks, *block), bf),
                vmem((chip_blocks, *block), bf),
                vmem((2, lanes, *block), bf),
                vmem((2, lanes, *block), bf),
                vmem((per_rank, *block), bf),
                vmem((per_rank, *block), bf),
                vmem((ranks, KV, ROWS, HEAD), bf),
                vmem((ranks * ROWS, blocks * tokens), f32),
                vmem((ranks, KV, ROWS, HEAD), f32),
                vmem((ranks, ROWS, HEAD), f32),
                vmem((chips, KV, ROWS, HEAD), f32),
                vmem((chips, ROWS, HEAD), f32),
                vmem((chips, KV, ROWS, HEAD), bf),
                vmem((chips, ROWS, HEAD), f32),
                vmem((chips, KV, ROWS, HEAD), bf),
                vmem((chips, ROWS, HEAD), f32),
                pltpu.SMEM((2, lanes), jnp.int32),
                vmem(queries.shape, f32),
                dma((6,)),
                dma,
                dma,
                dma((2, lanes, PIECES)),
                dma((2, lanes, PIECES)),
                dma((2,)),
                dma((2,)),
                dma((2, chips)),
                dma((2, chips)),
                dma,
                dma,
                dma,
            ],
            compiler_params=pltpu.CompilerParams(
                collective_id=1 + number, has_side_effects=True, vmem_limit_bytes=VMEM_BYTES
            ),
            name="exchange",
        )(*operands)

    pick, gathered_queries, other = pl.pallas_call(
        functools.partial(load_kernel, chips, chip_blocks, rank_slots, choices),
        out_shape=(
            jax.ShapeDtypeStruct((1,), jnp.int32),
            jax.ShapeDtypeStruct((chips, KV, ROWS, HEAD), bf),
            jax.ShapeDtypeStruct((per_rank, *block), bf),
        ),
        in_specs=[smem_spec, vmem_spec, any_spec, any_spec],
        out_specs=(smem_spec, vmem_spec, vmem_spec),
        scratch_shapes=[
            vmem((lax.axis_size("grp"), 8, HEAD), jnp.int32),
            vmem((KV, ROWS, HEAD), f32),
            vmem((KV, ROWS, HEAD), bf),
            dma((lax.axis_size("grp"),)),
            dma((lax.axis_size("grp"),)),
            dma((chips,)),
            dma((chips,)),
            dma,
            dma,
        ],
        compiler_params=pltpu.CompilerParams(
            collective_id=0, has_side_effects=True, vmem_limit_bytes=VMEM_BYTES
        ),
        name="load",
    )(spill_slots, queries, prefill_keys, prefill_values)
    att, newk, newv = lax.switch(
        pick[0],
        [functools.partial(exchange, number, lanes) for number, lanes in enumerate(choices)],
        context_lengths, block_table, spill_slots, gathered_queries, other,
        prefill_keys, prefill_values, cache_keys, pool_values_prior,
    )

    pool_keys, pool_values, att = pl.pallas_call(
        place_kernel,
        out_shape=(
            jax.ShapeDtypeStruct(cache_keys.shape, bf),
            jax.ShapeDtypeStruct(cache_keys.shape, bf),
            jax.ShapeDtypeStruct(att.shape, bf),
        ),
        in_specs=[smem_spec, smem_spec] + [any_spec] * 4 + [vmem_spec],
        out_specs=(any_spec, any_spec, vmem_spec),
        scratch_shapes=[vmem((2, rank_slots, *block), bf), dma((2, rank_slots)), dma((2, rank_slots))],
        compiler_params=pltpu.CompilerParams(vmem_limit_bytes=VMEM_BYTES),
        name="place",
    )(spill_slots, first.reshape(1), cache_keys, pool_values_prior, newk, newv, att)
    return att, pool_keys, pool_values


def solution(mesh):
    both = ("grp", "blk")
    return jax.shard_map(
        per_device,
        mesh=mesh,
        in_specs=(P(both, None),) + (P(both, None, None),) * 4 + (P("grp"), P("grp", None), P("grp")),
        out_specs=(P(both, None), P(both, None, None), P(both, None, None)),
        check_vma=False,
    )
```
